128 devices in a mesh: member: 16 (over y_lo, z, core), tile: 8 (over x, y_hi).
Axes of the slice: x: 4, y: 4 (y_hi: 2, y_lo: 2; y = y_hi * 2 + y_lo), z: 4, core: 2. Of those that a mesh axis runs over, the one named last changes fastest.
Arguments:
- ensemble: float32 [256, 4, 32, 3072], P('member', None, None, 'tile'), may hold values from -6 to 6
- kappa: float32 [4, 32, 3072], P(None, None, 'tile'), may hold values from 0.02 to 0.15
- advect: float32 [4], replicated, may hold values from 0.1 to 0.35
- observed: float32 [4, 16, 8, 768], P(None, 'member', 'tile'), may hold values from -6 to 6
- counts: int32 [4, 16, 8, 768], P(None, 'member', 'tile'), may hold values from 0 to 3
Outputs:
- analysis: float32 [256, 4, 32, 3072], P('member', None, None, 'tile')
The draws below stay inside these ranges and needn't reach their ends.
All inputs are finite; a program needn't handle non-finite values.
Results may differ from the reference program's by a relative error of at most 0.00023.
Values sent between devices are 32-bit elements; how exact they have to be, the bound alone decides.
A program may use at most 128 MiB of HBM per device.

```python
import jax
import jax.numpy as jnp
from jax import lax

LEV = 4
PROWS = 16
RBLK = 2
STEPS = 2
ITERS = 10
K = 256
CBLK = 8
PCOLS = 48
PCELLS = 768
GY = 32
GX = 3072
N_MEMBER = 16
N_TILE = 8


def touch_ends(array, stream_key, smallest, largest):
    index_at = [jax.random.randint(jax.random.fold_in(stream_key, axis), (), 0, length) for axis, length in enumerate(array.shape)]
    main_axis = array.shape.index(max(array.shape))
    beside = index_at[:main_axis] + [(index_at[main_axis] + 1) % array.shape[main_axis]] + index_at[main_axis + 1:]
    return array.at[tuple(index_at)].set(smallest).at[tuple(beside)].set(largest)


def steps_of(stream_key, extent, split, least, top_value):
    level, own = 1.0, jax.random.fold_in(stream_key, 6)
    for dim, shards_of in split:
        steps = jnp.exp(jax.random.uniform(jax.random.fold_in(own, dim), (shards_of,), jnp.float32, least / len(split), top_value / len(split)))
        level = level * jnp.repeat(steps, extent[dim] // shards_of).reshape([-1 if axis == dim else 1 for axis in range(len(extent))])
    return level


def normal_values(own_key, dims, scale, bound, pieces=(), kind=jnp.bfloat16):
    level = steps_of(own_key, dims, pieces, -0.22, 0.18) if pieces else 1.0
    drawn = jax.random.normal(own_key, dims, jnp.float32) * scale * level
    return jnp.minimum(jnp.maximum(drawn, -bound), bound).astype(kind)


def setup_inputs(seed: int = 0) -> dict:
    seeds = jax.random.split(jax.random.key(seed), 6)
    ensemble = normal_values(seeds[0], (K, LEV, GY, GX), 1.0, 6.0, ((0, 16), (3, 8)), jnp.float32)
    kappa = jnp.clip(0.02 + 0.13000001 * jax.random.uniform(seeds[1], (LEV, GY, GX), jnp.float32) ** steps_of(seeds[1], (LEV, GY, GX), ((2, 8),), -0.2, 0.2), 0.02, 0.15)
    advect = jnp.clip(jax.random.uniform(seeds[2], (LEV,), jnp.float32, 0.1, 0.35), 0.1, 0.35)
    observed = normal_values(seeds[3], (LEV, N_MEMBER, N_TILE, PCELLS), 1.0, 6.0, ((1, 16), (2, 8)), jnp.float32)
    counts = touch_ends(jax.random.randint(seeds[4], (LEV, N_MEMBER, N_TILE, PCELLS), 0, 4), jax.random.fold_in(seeds[4], 1), 0, 3).astype(jnp.int32)
    return {"ensemble": ensemble, "kappa": kappa, "advect": advect, "observed": observed, "counts": counts}


def advance(field, kappa, advect):
    east = jnp.roll(field, -1, axis=3)
    west = jnp.roll(field, 1, axis=3)
    padded = jnp.pad(field, ((0, 0), (0, 0), (1, 1), (0, 0)))
    north = padded[:, :, 2:]
    south = padded[:, :, :-2]
    laplace = east + west + north + south - 4.0 * field
    return field + kappa * laplace + advect[:, None, None] * (west - field)

def analyse_patch(background, observed, counts):
    members = background.shape[0]
    highest = lax.Precision.HIGHEST
    mean = lax.optimization_barrier(jnp.mean(background, axis=0))
    pert = background - mean
    prec = counts.astype(jnp.float32) * 0.25
    gram = jnp.dot(pert * prec, pert.T, precision=highest) / (members - 1)
    identity = jnp.eye(members, dtype=jnp.float32)
    system = identity + gram
    scale = jnp.sqrt(jnp.sum(system * system))

    def newton(step, carry):
        root, inverse = carry
        factor = 1.5 * identity - 0.5 * jnp.dot(inverse, root, precision=highest)
        return (jnp.dot(root, factor, precision=highest), jnp.dot(factor, inverse, precision=highest))
    root, inverse = lax.fori_loop(0, ITERS, newton, (system / scale, identity))
    half = inverse / jnp.sqrt(scale)
    full = jnp.dot(half, half, precision=highest)
    drive = jnp.dot(pert, prec * (observed - mean), precision=highest) / (members - 1)
    mean_w = jnp.dot(full, drive, precision=highest)
    weights = half + mean_w[:, None]
    return mean + jnp.dot(weights.T, pert, precision=highest)

def reference(ensemble, kappa, advect, observed, counts):
    field = ensemble
    for step in range(STEPS):
        field = advance(field, kappa, advect)
    tiles = N_TILE
    blocks = field.reshape(K, LEV, RBLK, PROWS, tiles, CBLK, PCOLS).transpose(1, 2, 5, 4, 0, 3, 6)
    blocks = blocks.reshape(LEV * RBLK * CBLK * tiles, K, PCELLS)
    obs_blocks = observed.reshape(-1, PCELLS)
    cnt_blocks = counts.reshape(-1, PCELLS)
    result = lax.map(lambda item: analyse_patch(item[0], item[1], item[2]), (blocks, obs_blocks, cnt_blocks))
    result = result.reshape(LEV, RBLK, CBLK, tiles, K, PROWS, PCOLS).transpose(4, 0, 1, 5, 3, 2, 6)
    return result.reshape(K, LEV, GY, GX)
```

```python
import jax
import jax.numpy as jnp
from jax import lax
from jax.experimental import pallas as pl
from jax.experimental.pallas import tpu as pltpu
from jax.sharding import PartitionSpec as P

MESH = pl.DeviceIdType.MESH
F32 = jnp.float32
BF16 = jnp.bfloat16
LEV = 4
ROWS = 32
WIDE = 384
CELLS = 768
COLS = 48
LANES = 128
MINE = 16
K = 256
PEERS = 16
TILES = 8
ITERS = 10


def loop(count, body):
    def step(i, carry):
        body(i)
        return carry

    lax.fori_loop(0, count, step, 0)


def split3(a):
    a0 = a.astype(BF16)
    rest = a - a0.astype(F32)
    a1 = rest.astype(BF16)
    return a0, a1, (rest - a1.astype(F32)).astype(BF16)


def mm(a, b):
    return jnp.dot(a, b, preferred_element_type=F32)


def mm_t(a, b):
    return lax.dot_general(a, b, (((1,), (1,)), ((), ())), preferred_element_type=F32)


def product(a, b):
    return mm(a[0], b[0]) + (
        (mm(a[0], b[1]) + mm(a[1], b[0]))
        + (mm(a[1], b[1]) + mm(a[0], b[2]) + mm(a[2], b[0]))
    )


def swap_blocks(rows):
    turned = [pltpu.roll(r, COLS * i, 1) if i else r for i, r in enumerate(rows)]
    lane = lax.broadcasted_iota(jnp.int32, (8, LANES), 1)
    result = []
    for d in range(8):
        parts = []
        for t in range(3):
            low, high = LANES * t, LANES * (t + 1)
            first, last = low // COLS, (high - 1) // COLS
            here = [turned[(p - d) % 8][:, low:high] for p in range(first, last + 1)]
            value = here[-1]
            for p in range(last - 1, first - 1, -1):
                value = jnp.where(lane < COLS * (p + 1) - low, here[p - first], value)
            parts.append(value)
        whole = jnp.concatenate(parts, axis=1)
        result.append(pltpu.roll(whole, WIDE - COLS * d, 1) if d else whole)
    return result


def kernel(
    ens, kap, adv, obs, cnt, out,
    ensv, kapv, send_w, send_e, recv_e, recv_w, edge, kedge, u0, u1,
    snd, rcv, pert, ph, pm, pl_, qh, ql, drive, inv, root, ana, ret, outv,
    in_sem, halo_ss, halo_rs, fwd_ss, fwd_rs, own_sem, back_ss, back_rs, out_sem,
):
    me = lax.axis_index("member")
    tile = lax.axis_index("tile")
    east = lax.rem(tile + 1, TILES)
    west = lax.rem(tile + TILES - 1, TILES)

    loads = [
        pltpu.make_async_copy(ens.at[:, pl.ds(LANES * t, LANES)], ensv.at[t], in_sem.at[t]) for t in range(3)
    ] + [
        pltpu.make_async_copy(kap.at[:, pl.ds(LANES * t, LANES)], kapv.at[t], in_sem.at[3 + t]) for t in range(3)
    ]
    for load in loads:
        load.start()

    barrier = pltpu.get_barrier_semaphore()

    def greet(k):
        peer = lax.rem(me + k + 1, PEERS)
        pl.semaphore_signal(barrier, inc=1, device_id={"member": peer}, device_id_type=MESH)

    loop(PEERS - 1, greet)
    for side in (east, west):
        pl.semaphore_signal(barrier, inc=1, device_id={"tile": side}, device_id_type=MESH)

    zero_row = jnp.zeros((8, 512), F32)
    for u in (u0, u1):
        u[0] = zero_row
        u[ROWS + 1] = zero_row
    for load in loads:
        load.wait()

    lane = lax.broadcasted_iota(jnp.int32, (8, LANES), 1)

    def gather_edges(rows_of, blocks):
        def block(b, carry):
            first, last = carry
            fb = jnp.zeros((8, LANES), F32)
            lb = jnp.zeros((8, LANES), F32)
            for i in range(8):
                head, tail = rows_of(b * 8 + i)
                if i:
                    head, tail = pltpu.roll(head, 4 * i, 1), pltpu.roll(tail, 4 * i, 1)
                fb = jnp.where(lane // 4 == i, head, fb)
                lb = jnp.where(((lane + 2) % LANES) // 4 == i, tail, lb)
            fb = pltpu.roll(fb, 32 * b, 1)
            lb = pltpu.roll(lb, 32 * b, 1)
            first = jnp.where(lane // 32 == b, fb, first)
            last = jnp.where(((lane + 2) % LANES) // 32 == b, lb, last)
            return first, last

        blank = jnp.zeros((8, LANES), F32)
        return lax.fori_loop(0, blocks, block, (blank, blank))

    def edges_of(j):
        l, g = j // 2, lax.rem(j, 2)

        def rows_of(y):
            at = pl.ds(g * 1024 + l * ROWS + y, 8, stride=128)
            return ensv[0, at, :], ensv[2, at, :]

        first, last = gather_edges(rows_of, 4)
        send_w[j] = first
        send_e[j] = last

    loop(2 * LEV, edges_of)

    def kappa_rows(y):
        at = pl.ds(y, 8, stride=16)
        return kapv[0, at, :], kapv[2, at, :]

    first, last = gather_edges(kappa_rows, 2)
    send_w[2 * LEV] = first
    send_e[2 * LEV] = last

    pl.semaphore_wait(barrier, PEERS + 1)

    to_west = pltpu.make_async_remote_copy(
        send_w, recv_e, halo_ss.at[0], halo_rs.at[0], device_id={"tile": west}, device_id_type=MESH)
    to_east = pltpu.make_async_remote_copy(
        send_e, recv_w, halo_ss.at[1], halo_rs.at[1], device_id={"tile": east}, device_id_type=MESH)
    to_west.start()
    to_east.start()
    to_west.wait()
    to_east.wait()

    for j in range(2 * LEV + 1):
        edge[j] = jnp.where(lane % 4 < 2, recv_e[j], recv_w[j])

    def kappa_edges(r):
        l, q = r // 2, lax.rem(r, 2)
        row = jnp.broadcast_to(edge[2 * LEV, pl.ds(r, 1), :], (8, LANES))
        for i in range(16):
            kedge[l * ROWS + q * 16 + i] = pltpu.roll(row, LANES - 4 * i, 1) if i else row

    loop(2 * LEV, kappa_edges)

    def forward(l, k):
        peer = lax.rem(me + k + 1, PEERS)
        return pltpu.make_async_remote_copy(
            snd.at[l, peer], rcv.at[l, pl.ds(me * MINE, MINE), :], fwd_ss.at[l], fwd_rs.at[l],
            device_id={"member": peer}, device_id_type=MESH)

    def forward_own(l):
        return pltpu.make_async_copy(snd.at[l, me], rcv.at[l, pl.ds(me * MINE, MINE), :], own_sem.at[l])

    def backward(l, k):
        peer = lax.rem(me + k + 1, PEERS)
        return pltpu.make_async_remote_copy(
            ana.at[l, pl.ds(peer * MINE, MINE), :], ret.at[l, pl.ds(me * MINE, MINE), :],
            back_ss.at[l], back_rs.at[l], device_id={"member": peer}, device_id_type=MESH)

    def backward_own(l):
        at = pl.ds(me * MINE, MINE)
        return pltpu.make_async_copy(ana.at[l, at, :], ret.at[l, at, :], own_sem.at[LEV + l])

    def wait_bytes(ref, sem):
        pltpu.make_async_copy(ref, ref, sem).wait()

    def advanced(u, l, b, speed):
        rows = [u[8 * b + i] for i in range(10)]
        result = []
        for i in range(8):
            south, here, north = rows[i], rows[i + 1], rows[i + 2]
            at = l * ROWS + 8 * b + i
            kappa = jnp.concatenate(
                [jnp.broadcast_to(kapv[t, pl.ds(at, 1), :], (8, LANES)) for t in range(3)] + [kedge[at]], axis=1)
            east_cell = pltpu.roll(here, 511, 1)
            west_cell = pltpu.roll(here, 1, 1)
            laplace = east_cell + west_cell + north + south - 4.0 * here
            result.append(here + kappa * laplace + speed * (west_cell - here))
        return result

    def steps_of(l):
        speed = adv[l]

        def group(g):
            def fill(b):
                halo = pltpu.roll(edge[2 * l + g], lax.rem(LANES - 32 * b, LANES), 1)
                for i in range(8):
                    y = 8 * b + i
                    for t in range(3):
                        row = ensv[t, pl.ds(g * 1024 + l * ROWS + y, 8, stride=128), :]
                        u0[y + 1, :, LANES * t:LANES * (t + 1)] = row
                    u0[y + 1, :, WIDE:512] = pltpu.roll(halo, LANES - 4 * i, 1) if i else halo

            loop(4, fill)

            def one(b):
                for i, row in enumerate(advanced(u0, l, b, speed)):
                    u1[8 * b + i + 1] = row

            loop(4, one)

            def two(b):
                rows = [row[:, 0:WIDE] for row in advanced(u1, l, b, speed)]
                r, h = b // 2, lax.rem(b, 2)
                for c, patch in enumerate(swap_blocks(rows)):
                    snd[l, r * 8 + c, pl.ds(pl.multiple_of(g * 8, 8), 8),
                        pl.ds(pl.multiple_of(h * WIDE, LANES), WIDE)] = patch

            loop(4, two)

        loop(2, group)
        forward_own(l).start()
        loop(PEERS - 1, lambda k: forward(l, k).start())

    loop(LEV, steps_of)

    def analyse(l):
        forward_own(l).wait()
        wait_bytes(rcv.at[l, pl.ds(0, K - MINE), :], fwd_rs.at[l])

        total = jnp.zeros((8, CELLS), F32)

        def add_rows(i, total):
            block = rcv[l, pl.ds(pl.multiple_of(i * 32, 32), 32), :]
            return total + ((block[0:8] + block[8:16]) + (block[16:24] + block[24:32]))

        total = lax.fori_loop(0, 8, add_rows, total)
        mean = jnp.sum(total, axis=0, keepdims=True) * (1.0 / K)
        prec = cnt[pl.ds(l, 1), :].astype(F32) * 0.25
        weight = prec * (obs[pl.ds(l, 1), :] - mean) * (1.0 / (K - 1))

        def centre(i):
            at = pl.ds(pl.multiple_of(i * 32, 32), 32)
            block = rcv[l, at, :] - mean
            pert[at, :] = block
            p0, p1, p2 = split3(block)
            ph[at, :] = p0
            pm[at, :] = p1
            pl_[at, :] = p2
            scaled = block * prec
            q0 = scaled.astype(BF16)
            qh[at, :] = q0
            ql[at, :] = (scaled - q0.astype(F32)).astype(BF16)
            drive[at, :] = jnp.sum(block * weight, axis=1, keepdims=True)

        loop(8, centre)

        gram = mm_t(qh[...], ph[...]) + (mm_t(qh[...], pm[...]) + mm_t(ql[...], ph[...]))
        eye = jnp.where(
            lax.broadcasted_iota(jnp.int32, (K, K), 0) == lax.broadcasted_iota(jnp.int32, (K, K), 1), 1.0, 0.0)
        system = eye + gram * (1.0 / (K - 1))
        scale = jnp.sqrt(jnp.sum(jnp.sum(system * system, axis=1, keepdims=True), axis=0, keepdims=True))
        first = system * (1.0 / scale)
        factor = 1.5 * eye - 0.5 * first
        inv[...] = factor
        root[...] = product(split3(first), split3(factor))

        def newton(i):
            held, base = split3(inv[...]), split3(root[...])
            factor = split3(1.5 * eye - 0.5 * product(held, base))
            inv[...] = product(held, factor)
            root[...] = product(base, factor)

        loop(ITERS - 2, newton)
        held, base = split3(inv[...]), split3(root[...])
        factor = split3(1.5 * eye - 0.5 * product(held, base))
        half = product(held, factor) * lax.rsqrt(scale)
        inv[...] = half

        turned = jnp.sum(half * drive[...], axis=0, keepdims=True)
        drive[...] = jnp.sum(half * turned, axis=1, keepdims=True)

        def shift(i, total):
            at = pl.ds(pl.multiple_of(i * 32, 32), 32)
            block = pert[at, :] * drive[at, :]
            return total + ((block[0:8] + block[8:16]) + (block[16:24] + block[24:32]))

        total = lax.fori_loop(0, 8, shift, jnp.zeros((8, CELLS), F32))
        centre_row = mean + jnp.sum(total, axis=0, keepdims=True)
        h0, h1, h2 = split3(half)
        for c in range(3):
            at = slice(256 * c, 256 * (c + 1))
            cells = (ph[:, at], pm[:, at], pl_[:, at])
            ana[l, :, at] = centre_row[:, at] + product((h0, h1, h2), cells)

        backward_own(l).start()
        loop(PEERS - 1, lambda k: backward(l, k).start())

    loop(LEV, analyse)

    def finish(l):
        backward_own(l).wait()
        wait_bytes(ret.at[l, pl.ds(0, K - MINE), :], back_rs.at[l])

        def part(j):
            g, b = j // 4, lax.rem(j, 4)
            r, h = b // 2, lax.rem(b, 2)
            patches = [
                ret[l, pl.ds(pl.multiple_of((r * 8 + c) * MINE + g * 8, 8), 8),
                    pl.ds(pl.multiple_of(h * WIDE, LANES), WIDE)]
                for c in range(8)
            ]
            for i, row in enumerate(swap_blocks(patches)):
                for t in range(3):
                    outv[t, pl.ds(g * 1024 + l * ROWS + 8 * b + i, 8, stride=128), :] = row[:, LANES * t:LANES * (t + 1)]

        loop(8, part)

    loop(LEV, finish)
    stores = [
        pltpu.make_async_copy(outv.at[t], out.at[:, pl.ds(LANES * t, LANES)], out_sem.at[t]) for t in range(3)
    ]
    for store in stores:
        store.start()

    def drain(l):
        wait_bytes(snd.at[l, pl.ds(0, PEERS - 1)], fwd_ss.at[l])
        wait_bytes(ana.at[l, pl.ds(0, K - MINE), :], back_ss.at[l])

    loop(LEV, drain)
    for store in stores:
        store.wait()


def on_device(ensemble, kappa, advect, observed, counts):
    every = MINE * LEV * ROWS
    scratch = [
        pltpu.VMEM((3, every, LANES), F32),
        pltpu.VMEM((3, LEV * ROWS, LANES), F32),
        *[pltpu.VMEM((2 * LEV + 1, 8, LANES), F32)] * 5,
        pltpu.VMEM((LEV * ROWS, 8, LANES), F32),
        *[pltpu.VMEM((ROWS + 2, 8, 512), F32)] * 2,
        pltpu.VMEM((LEV, PEERS, MINE, CELLS), F32),
        pltpu.VMEM((LEV, K, CELLS), F32),
        pltpu.VMEM((K, CELLS), F32),
        *[pltpu.VMEM((K, CELLS), BF16)] * 5,
        pltpu.VMEM((K, 1), F32),
        *[pltpu.VMEM((K, K), F32)] * 2,
        pltpu.VMEM((LEV, K, CELLS), F32),
        pltpu.VMEM((LEV, K, CELLS), F32),
        pltpu.VMEM((3, every, LANES), F32),
        pltpu.SemaphoreType.DMA((6,)),
        *[pltpu.SemaphoreType.DMA((2,))] * 2,
        *[pltpu.SemaphoreType.DMA((LEV,))] * 2,
        pltpu.SemaphoreType.DMA((2 * LEV,)),
        *[pltpu.SemaphoreType.DMA((LEV,))] * 2,
        pltpu.SemaphoreType.DMA((3,)),
    ]
    vmem = pl.BlockSpec(memory_space=pltpu.VMEM)
    hbm = pl.BlockSpec(memory_space=pl.ANY)
    result = pl.pallas_call(
        kernel,
        out_shape=jax.ShapeDtypeStruct((every, WIDE), F32),
        in_specs=[
            hbm, hbm, pl.BlockSpec(memory_space=pltpu.SMEM), vmem, vmem],
        out_specs=pl.BlockSpec(memory_space=pl.ANY),
        scratch_shapes=scratch,
        compiler_params=pltpu.CompilerParams(
            collective_id=0, has_side_effects=True, vmem_limit_bytes=56 * 1024 * 1024),
        name="analysis",
    )(
        ensemble.reshape(every, WIDE),
        kappa.reshape(LEV * ROWS, WIDE),
        advect,
        observed.reshape(LEV, CELLS),
        counts.reshape(LEV, CELLS),
    )
    return result.reshape(MINE, LEV, ROWS, WIDE)


def solution(mesh):
    in_specs = (
        P("member", None, None, "tile"),
        P(None, None, "tile"),
        P(),
        P(None, "member", "tile", None),
        P(None, "member", "tile", None),
    )
    return jax.shard_map(
        on_device, mesh=mesh, in_specs=in_specs, out_specs=P("member", None, None, "tile"), check_vma=False
    )
```

```python
import jax
import jax.numpy as jnp
from jax import lax
from jax.experimental import pallas as pl
from jax.experimental.pallas import tpu as pltpu
from jax.sharding import PartitionSpec as P

MESH = pl.DeviceIdType.MESH
F32 = jnp.float32
BF16 = jnp.bfloat16
LEV = 4
ROWS = 32
PAD = ROWS + 2
WIDE = 384
CELLS = 768
COLS = 48
LANES = 128
MINE = 16
FIELDS = 24
CHUNK = 64
K = 256
PEERS = 16
TILES = 8
ITERS = 10


def loop(count, body):
    def step(i, carry):
        body(i)
        return carry

    lax.fori_loop(0, count, step, 0)


def split3(a):
    a0 = a.astype(BF16)
    rest = a - a0.astype(F32)
    a1 = rest.astype(BF16)
    return a0, a1, (rest - a1.astype(F32)).astype(BF16)


def mm(a, b):
    return jnp.dot(a, b, preferred_element_type=F32)


def mm_t(a, b):
    return lax.dot_general(a, b, (((1,), (1,)), ((), ())), preferred_element_type=F32)


def product(a, b):
    return mm(a[0], b[0]) + (
        (mm(a[0], b[1]) + mm(a[1], b[0]))
        + (mm(a[1], b[1]) + mm(a[0], b[2]) + mm(a[2], b[0]))
    )


def sheared(arrays):
    lane = lax.broadcasted_iota(jnp.int32, (MINE, LANES), 1)
    result = []
    for d in range(8):
        parts = []
        for t in range(3):
            low, high = LANES * t, LANES * (t + 1)
            first, last = low // COLS, (high - 1) // COLS
            here = [arrays[(p - d) % 8][:, low:high] for p in range(first, last + 1)]
            value = here[-1]
            for p in range(last - 1, first - 1, -1):
                value = jnp.where(lane < COLS * (p + 1) - low, here[p - first], value)
            parts.append(value)
        result.append(jnp.concatenate(parts, axis=1))
    return result


def turned(array, shift):
    shift %= array.shape[1]
    return pltpu.roll(array, shift, 1) if shift else array


def moved(here, east, west, north, south, kappa, speed):
    return here + kappa * (east + west + north + south - 4.0 * here) + speed * (west - here)


def kernel(
    ens, kap, adv, obs, cnt, out,
    ensv, send_w, send_e, recv_e, recv_w, mend_w, mend_e, u1,
    snd, rcv, pert, ph, pm, pl_, qh, ql, drive, inv, root, ana, ret, outv,
    in_sem, halo_ss, halo_rs, fwd_ss, fwd_rs, own_sem, back_ss, back_rs, out_sem,
):
    me = lax.axis_index("member")
    tile = lax.axis_index("tile")
    east = lax.rem(tile + 1, TILES)
    west = lax.rem(tile + TILES - 1, TILES)
    inner = pl.ds(1, ROWS)

    def load_levels(part, base, count):
        levels = pl.ds(base, count)

        def member(m):
            pltpu.make_async_copy(
                ens.at[m, levels], ensv.at[levels, inner, m, :], in_sem.at[part]).start()

        def copy_kappa(m):
            pltpu.make_async_copy(
                kap.at[levels], ensv.at[levels, inner, MINE + m, :], in_sem.at[part]).start()

        loop(MINE, member)
        loop(FIELDS - MINE, copy_kappa)

    load_levels(0, 0, 1)
    load_levels(1, 1, LEV - 1)

    barrier = pltpu.get_barrier_semaphore()

    def greet(k):
        peer = lax.rem(me + k + 1, PEERS)
        pl.semaphore_signal(barrier, inc=1, device_id={"member": peer}, device_id_type=MESH)

    loop(PEERS - 1, greet)
    for side in (east, west):
        pl.semaphore_signal(barrier, inc=1, device_id={"tile": side}, device_id_type=MESH)

    def clear(l):
        for y in (0, ROWS + 1):
            ensv[l, y] = jnp.zeros((FIELDS, WIDE), F32)
            u1[l, y] = jnp.zeros((MINE, WIDE), F32)

    loop(LEV, clear)

    def wait_bytes(ref, sem):
        pltpu.make_async_copy(ref, ref, sem).wait()

    wait_bytes(ensv.at[pl.ds(0, 1), inner], in_sem.at[0])

    def step_one(l, b):
        rows = [ensv[l, 8 * b + i, 0:MINE] for i in range(10)]
        speed = adv[l]
        for i in range(8):
            south, here, north = rows[i:i + 3]
            kappa = ensv[l, 8 * b + i + 1, MINE:FIELDS]
            kappa = jnp.concatenate([kappa, kappa], axis=0)
            u1[l, 8 * b + i + 1] = moved(here, turned(here, -1), turned(here, 1), north, south, kappa, speed)

    def step_two(l, b):
        rows = [u1[l, 8 * b + i] for i in range(10)]
        speed = adv[l]
        done = []
        for i in range(8):
            south, here, north = rows[i:i + 3]
            kappa = ensv[l, 8 * b + i + 1, MINE:FIELDS]
            kappa = jnp.concatenate([kappa, kappa], axis=0)
            row = moved(here, turned(here, -1), turned(here, 1), north, south, kappa, speed)
            done.append(turned(row, COLS * i))
        r, h = b // 2, lax.rem(b, 2)
        for c, patch in enumerate(sheared(done)):
            snd[l, r * 8 + c, :, pl.ds(pl.multiple_of(h * WIDE, LANES), WIDE)] = patch

    loop(4, lambda b: step_one(0, b))
    wait_bytes(ensv.at[pl.ds(1, LEV - 1), inner], in_sem.at[1])

    lane = lax.broadcasted_iota(jnp.int32, (FIELDS, LANES), 1)

    def edges_of(l):
        first = jnp.zeros((FIELDS, LANES), F32)
        last = jnp.zeros((FIELDS, LANES), F32)
        for y in range(ROWS):
            ends = jnp.where(lane < 64, ensv[l, y + 1, :, 0:LANES], ensv[l, y + 1, :, 2 * LANES:3 * LANES])
            ends = turned(ends, 4 * y)
            first = jnp.where(lane // 4 == y, ends, first)
            last = jnp.where(lane // 4 == (y - 1) % ROWS, ends, last)
        send_w[l] = first
        send_e[l] = turned(last, 4)

    loop(LEV, edges_of)
    pl.semaphore_wait(barrier, PEERS + 1)

    to_west = pltpu.make_async_remote_copy(
        send_w, recv_e, halo_ss.at[0], halo_rs.at[0], device_id={"tile": west}, device_id_type=MESH)
    to_east = pltpu.make_async_remote_copy(
        send_e, recv_w, halo_ss.at[1], halo_rs.at[1], device_id={"tile": east}, device_id_type=MESH)
    to_west.start()
    to_east.start()

    def forward(l, peer):
        return pltpu.make_async_remote_copy(
            snd.at[l, peer], rcv.at[l, pl.ds(me * MINE, MINE), :], fwd_ss.at[l], fwd_rs.at[l],
            device_id={"member": peer}, device_id_type=MESH)

    def forward_own(l):
        return pltpu.make_async_copy(snd.at[l, me], rcv.at[l, pl.ds(me * MINE, MINE), :], own_sem.at[l])

    def backward(l, k):
        peer = lax.rem(me + k + 1, PEERS)
        return pltpu.make_async_remote_copy(
            ana.at[l, pl.ds(peer * MINE, MINE), :], ret.at[l, pl.ds(me * MINE, MINE), :],
            back_ss.at[l], back_rs.at[l], device_id={"member": peer}, device_id_type=MESH)

    def backward_own(l):
        at = pl.ds(me * MINE, MINE)
        return pltpu.make_async_copy(ana.at[l, at, :], ret.at[l, at, :], own_sem.at[LEV + l])

    def send(l, wanted):
        def one(k):
            peer = lax.rem(me + k, PEERS)
            column = lax.rem(peer, 8)
            outer = jnp.logical_or(column == 0, column == 7)

            @pl.when(outer if wanted else jnp.logical_not(outer))
            def _():
                @pl.when(k == 0)
                def _():
                    forward_own(l).start()

                @pl.when(k > 0)
                def _():
                    forward(l, peer).start()

        loop(PEERS, one)

    def compact(a, b, ka, kb, speed, want_a, want_b):
        place = lax.broadcasted_iota(jnp.int32, a.shape, 1)
        slot = place % 4

        def sides(x):
            south = jnp.where(place < 4, 0.0, pltpu.roll(x, 4, 1))
            north = jnp.where(place >= LANES - 4, 0.0, pltpu.roll(x, LANES - 4, 1))
            return north, south

        new_a = new_b = None
        if want_a:
            after = jnp.where(slot == 3, pltpu.roll(b, 3, 1), pltpu.roll(a, LANES - 1, 1))
            new_a = moved(a, after, pltpu.roll(a, 1, 1), *sides(a), ka, speed)
        if want_b:
            before = jnp.where(slot == 0, pltpu.roll(a, LANES - 3, 1), pltpu.roll(b, 1, 1))
            new_b = moved(b, pltpu.roll(b, LANES - 1, 1), before, *sides(b), kb, speed)
        return new_a, new_b

    def mend_edges(l):
        speed = adv[l]

        def parts(ref):
            kappa = ref[l, MINE:FIELDS]
            return ref[l, 0:MINE], jnp.concatenate([kappa, kappa], axis=0)

        (a, ka), (b, kb) = parts(recv_w), parts(send_w)
        a, b = compact(a, b, ka, kb, speed, True, True)
        mend_w[l] = compact(a, b, ka, kb, speed, False, True)[1]
        (a, ka), (b, kb) = parts(send_e), parts(recv_e)
        a, b = compact(a, b, ka, kb, speed, True, True)
        mend_e[l] = compact(a, b, ka, kb, speed, True, False)[0]

    def insert_edges(l):
        place = lax.broadcasted_iota(jnp.int32, (MINE, LANES), 1)
        for mend, c, cell in ((mend_w, 0, 0), (mend_e, 7, COLS - 2)):
            values = mend[l]
            for b in range(4):
                r, h = divmod(b, 2)
                tiles = [snd[l, r * 8 + c, :, WIDE * h + LANES * t:WIDE * h + LANES * (t + 1)] for t in range(3)]
                for i in range(8):
                    to = COLS * ((c + i) % 8) + cell
                    t, to = divmod(to, LANES)
                    source = 4 * (8 * b + i) + (2 if cell else 0)
                    value = turned(values, to - source)
                    tiles[t] = jnp.where(jnp.logical_or(place == to, place == to + 1), value, tiles[t])
                for t in range(3):
                    snd[l, r * 8 + c, :, WIDE * h + LANES * t:WIDE * h + LANES * (t + 1)] = tiles[t]

    def two_steps(l, follow):
        def body(b):
            step_two(l, b)
            if follow:
                step_one(l + 1, b)

        loop(4, body)

    def finish_edges(l):
        insert_edges(l)
        send(l, True)

    two_steps(0, True)
    send(0, False)
    two_steps(1, True)
    to_west.wait()
    to_east.wait()
    loop(LEV, mend_edges)
    finish_edges(0)
    send(1, False)
    finish_edges(1)

    two_steps(2, True)
    send(2, False)
    finish_edges(2)
    two_steps(3, False)
    send(3, False)
    finish_edges(3)

    order = COLS * lax.rem(me, 8)

    def ordered(row):
        row = jnp.broadcast_to(row, (8, CELLS))
        return jnp.concatenate(
            [pltpu.roll(row[:, WIDE * h:WIDE * (h + 1)], order, 1) for h in range(2)], axis=1)[0:1]

    def analyse(l):
        forward_own(l).wait()
        wait_bytes(rcv.at[l, pl.ds(0, K - MINE), :], fwd_rs.at[l])
        total = jnp.zeros((8, CELLS), F32)

        def add_rows(i, total):
            block = rcv[l, pl.ds(pl.multiple_of(i * CHUNK, CHUNK), CHUNK), :]
            return total + jnp.sum(block.reshape(CHUNK // 8, 8, CELLS), axis=0)

        total = lax.fori_loop(0, K // CHUNK, add_rows, total)
        mean = jnp.sum(total, axis=0, keepdims=True) * (1.0 / K)
        prec = ordered(cnt[l].astype(F32)) * 0.25
        weight = prec * (ordered(obs[l]) - mean) * (1.0 / (K - 1))

        def centre(i):
            at = pl.ds(pl.multiple_of(i * CHUNK, CHUNK), CHUNK)
            block = rcv[l, at, :] - mean
            pert[at, :] = block
            p0, p1, p2 = split3(block)
            ph[at, :] = p0
            pm[at, :] = p1
            pl_[at, :] = p2
            scaled = block * prec
            q0 = scaled.astype(BF16)
            qh[at, :] = q0
            ql[at, :] = (scaled - q0.astype(F32)).astype(BF16)
            drive[at, :] = jnp.sum(block * weight, axis=1, keepdims=True)

        loop(K // CHUNK, centre)

        gram = mm_t(qh[...], ph[...]) + (mm_t(qh[...], pm[...]) + mm_t(ql[...], ph[...]))
        eye = jnp.where(
            lax.broadcasted_iota(jnp.int32, (K, K), 0) == lax.broadcasted_iota(jnp.int32, (K, K), 1), 1.0, 0.0)
        system = eye + gram * (1.0 / (K - 1))
        scale = jnp.sqrt(jnp.sum(jnp.sum(system * system, axis=1, keepdims=True), axis=0, keepdims=True))
        first = system * (1.0 / scale)
        factor = 1.5 * eye - 0.5 * first
        inv[...] = factor
        root[...] = product(split3(first), split3(factor))

        def newton(i):
            held, base = split3(inv[...]), split3(root[...])
            factor = split3(1.5 * eye - 0.5 * product(held, base))
            inv[...] = product(held, factor)
            root[...] = product(base, factor)

        loop(ITERS - 2, newton)
        held, base = split3(inv[...]), split3(root[...])
        factor = split3(1.5 * eye - 0.5 * product(held, base))
        half = product(held, factor) * lax.rsqrt(scale)
        inv[...] = half

        turned = jnp.sum(half * drive[...], axis=0, keepdims=True)
        drive[...] = jnp.sum(half * turned, axis=1, keepdims=True)

        def shift(i, total):
            at = pl.ds(pl.multiple_of(i * CHUNK, CHUNK), CHUNK)
            block = pert[at, :] * drive[at, :]
            return total + jnp.sum(block.reshape(CHUNK // 8, 8, CELLS), axis=0)

        total = lax.fori_loop(0, K // CHUNK, shift, jnp.zeros((8, CELLS), F32))
        centre_row = mean + jnp.sum(total, axis=0, keepdims=True)
        h0, h1, h2 = split3(half)
        for c in range(3):
            at = slice(256 * c, 256 * (c + 1))
            cells = (ph[:, at], pm[:, at], pl_[:, at])
            ana[l, :, at] = centre_row[:, at] + product((h0, h1, h2), cells)

        backward_own(l).start()
        loop(PEERS - 1, lambda k: backward(l, k).start())

    loop(LEV, analyse)

    def finish(l):
        backward_own(l).wait()
        wait_bytes(ret.at[l, pl.ds(0, K - MINE), :], back_rs.at[l])

        def part(b):
            r, h = b // 2, lax.rem(b, 2)
            patches = [
                ret[l, pl.ds(pl.multiple_of((r * 8 + c) * MINE, MINE), MINE),
                    pl.ds(pl.multiple_of(h * WIDE, LANES), WIDE)]
                for c in range(8)
            ]
            for i, row in enumerate(sheared(patches)):
                outv[l, 8 * b + i] = turned(row, -COLS * i)

        loop(4, part)

        def member(m):
            pltpu.make_async_copy(outv.at[l, :, m, :], out.at[m, l], out_sem.at[l]).start()

        loop(MINE, member)

    loop(LEV, finish)

    def drain(l):
        wait_bytes(snd.at[l, pl.ds(0, PEERS - 1)], fwd_ss.at[l])
        wait_bytes(ana.at[l, pl.ds(0, K - MINE), :], back_ss.at[l])
        wait_bytes(outv.at[l], out_sem.at[l])

    loop(LEV, drain)


def on_device(ensemble, kappa, advect, observed, counts):
    scratch = [
        pltpu.VMEM((LEV, PAD, FIELDS, WIDE), F32),
        *[pltpu.VMEM((LEV, FIELDS, LANES), F32)] * 4,
        *[pltpu.VMEM((LEV, MINE, LANES), F32)] * 2,
        pltpu.VMEM((LEV, PAD, MINE, WIDE), F32),
        pltpu.VMEM((LEV, PEERS, MINE, CELLS), F32),
        pltpu.VMEM((LEV, K, CELLS), F32),
        pltpu.VMEM((K, CELLS), F32),
        *[pltpu.VMEM((K, CELLS), BF16)] * 5,
        pltpu.VMEM((K, 1), F32),
        *[pltpu.VMEM((K, K), F32)] * 2,
        pltpu.VMEM((LEV, K, CELLS), F32),
        pltpu.VMEM((LEV, K, CELLS), F32),
        pltpu.VMEM((LEV, ROWS, MINE, WIDE), F32),
        pltpu.SemaphoreType.DMA((2,)),
        *[pltpu.SemaphoreType.DMA((2,))] * 2,
        *[pltpu.SemaphoreType.DMA((LEV,))] * 2,
        pltpu.SemaphoreType.DMA((2 * LEV,)),
        *[pltpu.SemaphoreType.DMA((LEV,))] * 2,
        pltpu.SemaphoreType.DMA((LEV,)),
    ]
    vmem = pl.BlockSpec(memory_space=pltpu.VMEM)
    hbm = pl.BlockSpec(memory_space=pl.ANY)
    return pl.pallas_call(
        kernel,
        out_shape=jax.ShapeDtypeStruct((MINE, LEV, ROWS, WIDE), F32),
        in_specs=[hbm, hbm, pl.BlockSpec(memory_space=pltpu.SMEM), vmem, vmem],
        out_specs=hbm,
        scratch_shapes=scratch,
        compiler_params=pltpu.CompilerParams(
            collective_id=0, has_side_effects=True, vmem_limit_bytes=56 * 1024 * 1024),
        name="analysis",
    )(ensemble, kappa, advect, observed.reshape(LEV, 1, CELLS), counts.reshape(LEV, 1, CELLS))


def solution(mesh):
    in_specs = (
        P("member", None, None, "tile"),
        P(None, None, "tile"),
        P(),
        P(None, "member", "tile", None),
        P(None, "member", "tile", None),
    )
    return jax.shard_map(
        on_device, mesh=mesh, in_specs=in_specs, out_specs=P("member", None, None, "tile"), check_vma=False
    )
```

```python
import jax
import jax.numpy as jnp
from jax import lax
from jax.experimental import pallas as pl
from jax.experimental.pallas import tpu as pltpu
from jax.sharding import PartitionSpec as P

MESH = pl.DeviceIdType.MESH
F32 = jnp.float32
BF16 = jnp.bfloat16
LEV = 4
ROWS = 32
PAD = ROWS + 2
WIDE = 384
CELLS = 768
COLS = 48
LANES = 128
MINE = 16
FIELDS = 24
CHUNK = 64
K = 256
PEERS = 16
TILES = 8
ITERS = 10


def loop(count, body):
    def step(i, carry):
        body(i)
        return carry

    lax.fori_loop(0, count, step, 0)


def split3(a):
    a0 = a.astype(BF16)
    rest = a - a0.astype(F32)
    a1 = rest.astype(BF16)
    return a0, a1, (rest - a1.astype(F32)).astype(BF16)


def mm(a, b):
    return jnp.dot(a, b, preferred_element_type=F32)


def mm_t(a, b):
    return lax.dot_general(a, b, (((1,), (1,)), ((), ())), preferred_element_type=F32)


def product(a, b):
    return mm(a[0], b[0]) + (
        (mm(a[0], b[1]) + mm(a[1], b[0]))
        + (mm(a[1], b[1]) + mm(a[0], b[2]) + mm(a[2], b[0]))
    )


def sheared(arrays):
    lane = lax.broadcasted_iota(jnp.int32, (MINE, LANES), 1)
    result = []
    for d in range(8):
        parts = []
        for t in range(3):
            low, high = LANES * t, LANES * (t + 1)
            first, last = low // COLS, (high - 1) // COLS
            here = [arrays[(p - d) % 8][:, low:high] for p in range(first, last + 1)]
            value = here[-1]
            for p in range(last - 1, first - 1, -1):
                value = jnp.where(lane < COLS * (p + 1) - low, here[p - first], value)
            parts.append(value)
        result.append(jnp.concatenate(parts, axis=1))
    return result


def turned(array, shift):
    shift %= array.shape[1]
    return pltpu.roll(array, shift, 1) if shift else array


def moved(here, east, west, north, south, kappa, speed):
    return here + kappa * (east + west + north + south - 4.0 * here) + speed * (west - here)


def kernel(
    ens, kap, adv, obs, cnt, field,
    ensv, send_w, send_e, recv_e, recv_w, mend_w, mend_e, u1,
    snd, rcv, pert, ph, pm, pl_, qh, ql, drive, inv, root, ana, ret, outv,
    in_sem, halo_ss, halo_rs, fwd_ss, fwd_rs, own_sem, back_ss, back_rs, out_sem,
):
    me = lax.axis_index("member")
    tile = lax.axis_index("tile")
    east = lax.rem(tile + 1, TILES)
    west = lax.rem(tile + TILES - 1, TILES)
    inner = pl.ds(1, ROWS)

    def load_levels(part, base, count):
        levels = pl.ds(base, count)

        def member(m):
            pltpu.make_async_copy(
                ens.at[m, levels], ensv.at[levels, inner, m, :], in_sem.at[part]).start()

        def copy_kappa(m):
            pltpu.make_async_copy(
                kap.at[levels], ensv.at[levels, inner, MINE + m, :], in_sem.at[part]).start()

        loop(MINE, member)
        loop(FIELDS - MINE, copy_kappa)

    load_levels(0, 0, 1)
    load_levels(1, 1, LEV - 1)

    barrier = pltpu.get_barrier_semaphore()

    def greet(k):
        peer = lax.rem(me + k + 1, PEERS)
        pl.semaphore_signal(barrier, inc=1, device_id={"member": peer}, device_id_type=MESH)

    loop(PEERS - 1, greet)
    for side in (east, west):
        pl.semaphore_signal(barrier, inc=1, device_id={"tile": side}, device_id_type=MESH)

    def clear(l):
        for y in (0, ROWS + 1):
            ensv[l, y] = jnp.zeros((FIELDS, WIDE), F32)
            u1[l, y] = jnp.zeros((MINE, WIDE), F32)

    loop(LEV, clear)

    def wait_bytes(ref, sem):
        pltpu.make_async_copy(ref, ref, sem).wait()

    wait_bytes(ensv.at[pl.ds(0, 1), inner], in_sem.at[0])

    def step_one(l, b):
        rows = [ensv[l, 8 * b + i, 0:MINE] for i in range(10)]
        speed = adv[l]
        for i in range(8):
            south, here, north = rows[i:i + 3]
            kappa = ensv[l, 8 * b + i + 1, MINE:FIELDS]
            kappa = jnp.concatenate([kappa, kappa], axis=0)
            u1[l, 8 * b + i + 1] = moved(here, turned(here, -1), turned(here, 1), north, south, kappa, speed)

    def step_two(l, b):
        rows = [u1[l, 8 * b + i] for i in range(10)]
        speed = adv[l]
        done = []
        for i in range(8):
            south, here, north = rows[i:i + 3]
            kappa = ensv[l, 8 * b + i + 1, MINE:FIELDS]
            kappa = jnp.concatenate([kappa, kappa], axis=0)
            row = moved(here, turned(here, -1), turned(here, 1), north, south, kappa, speed)
            done.append(turned(row, COLS * i))
        r, h = b // 2, lax.rem(b, 2)
        for c, patch in enumerate(sheared(done)):
            snd[l, r * 8 + c, :, pl.ds(pl.multiple_of(h * WIDE, LANES), WIDE)] = patch

    loop(4, lambda b: step_one(0, b))
    wait_bytes(ensv.at[pl.ds(1, LEV - 1), inner], in_sem.at[1])

    lane = lax.broadcasted_iota(jnp.int32, (FIELDS, LANES), 1)

    def edges_of(l):
        first = jnp.zeros((FIELDS, LANES), F32)
        last = jnp.zeros((FIELDS, LANES), F32)
        for y in range(ROWS):
            ends = jnp.where(lane < 64, ensv[l, y + 1, :, 0:LANES], ensv[l, y + 1, :, 2 * LANES:3 * LANES])
            ends = turned(ends, 4 * y)
            first = jnp.where(lane // 4 == y, ends, first)
            last = jnp.where(lane // 4 == (y - 1) % ROWS, ends, last)
        send_w[l] = first
        send_e[l] = turned(last, 4)

    loop(LEV, edges_of)
    pl.semaphore_wait(barrier, PEERS + 1)

    to_west = pltpu.make_async_remote_copy(
        send_w, recv_e, halo_ss.at[0], halo_rs.at[0], device_id={"tile": west}, device_id_type=MESH)
    to_east = pltpu.make_async_remote_copy(
        send_e, recv_w, halo_ss.at[1], halo_rs.at[1], device_id={"tile": east}, device_id_type=MESH)
    to_west.start()
    to_east.start()

    def forward(l, peer):
        return pltpu.make_async_remote_copy(
            snd.at[l, peer], rcv.at[l, pl.ds(me * MINE, MINE), :], fwd_ss.at[l], fwd_rs.at[l],
            device_id={"member": peer}, device_id_type=MESH)

    def forward_own(l):
        return pltpu.make_async_copy(snd.at[l, me], rcv.at[l, pl.ds(me * MINE, MINE), :], own_sem.at[l])

    def backward(l, k):
        peer = lax.rem(me + k + 1, PEERS)
        return pltpu.make_async_remote_copy(
            ana.at[l, pl.ds(peer * MINE, MINE), :], ret.at[l, pl.ds(me * MINE, MINE), :],
            back_ss.at[l], back_rs.at[l], device_id={"member": peer}, device_id_type=MESH)

    def backward_own(l):
        at = pl.ds(me * MINE, MINE)
        return pltpu.make_async_copy(ana.at[l, at, :], ret.at[l, at, :], own_sem.at[LEV + l])

    def send(l, wanted):
        def one(k):
            peer = lax.rem(me + k, PEERS)
            column = lax.rem(peer, 8)
            outer = jnp.logical_or(column == 0, column == 7)

            @pl.when(outer if wanted else jnp.logical_not(outer))
            def _():
                @pl.when(k == 0)
                def _():
                    forward_own(l).start()

                @pl.when(k > 0)
                def _():
                    forward(l, peer).start()

        loop(PEERS, one)

    def compact(a, b, ka, kb, speed, want_a, want_b):
        place = lax.broadcasted_iota(jnp.int32, a.shape, 1)
        slot = place % 4

        def sides(x):
            south = jnp.where(place < 4, 0.0, pltpu.roll(x, 4, 1))
            north = jnp.where(place >= LANES - 4, 0.0, pltpu.roll(x, LANES - 4, 1))
            return north, south

        new_a = new_b = None
        if want_a:
            after = jnp.where(slot == 3, pltpu.roll(b, 3, 1), pltpu.roll(a, LANES - 1, 1))
            new_a = moved(a, after, pltpu.roll(a, 1, 1), *sides(a), ka, speed)
        if want_b:
            before = jnp.where(slot == 0, pltpu.roll(a, LANES - 3, 1), pltpu.roll(b, 1, 1))
            new_b = moved(b, pltpu.roll(b, LANES - 1, 1), before, *sides(b), kb, speed)
        return new_a, new_b

    def mend_edges(l):
        speed = adv[l]

        def parts(ref):
            kappa = ref[l, MINE:FIELDS]
            return ref[l, 0:MINE], jnp.concatenate([kappa, kappa], axis=0)

        (a, ka), (b, kb) = parts(recv_w), parts(send_w)
        a, b = compact(a, b, ka, kb, speed, True, True)
        mend_w[l] = compact(a, b, ka, kb, speed, False, True)[1]
        (a, ka), (b, kb) = parts(send_e), parts(recv_e)
        a, b = compact(a, b, ka, kb, speed, True, True)
        mend_e[l] = compact(a, b, ka, kb, speed, True, False)[0]

    def insert_edges(l):
        place = lax.broadcasted_iota(jnp.int32, (MINE, LANES), 1)
        for mend, c, cell in ((mend_w, 0, 0), (mend_e, 7, COLS - 2)):
            values = mend[l]
            for b in range(4):
                r, h = divmod(b, 2)
                tiles = [snd[l, r * 8 + c, :, WIDE * h + LANES * t:WIDE * h + LANES * (t + 1)] for t in range(3)]
                for i in range(8):
                    to = COLS * ((c + i) % 8) + cell
                    t, to = divmod(to, LANES)
                    source = 4 * (8 * b + i) + (2 if cell else 0)
                    value = turned(values, to - source)
                    tiles[t] = jnp.where(jnp.logical_or(place == to, place == to + 1), value, tiles[t])
                for t in range(3):
                    snd[l, r * 8 + c, :, WIDE * h + LANES * t:WIDE * h + LANES * (t + 1)] = tiles[t]

    def two_steps(l, follow):
        def body(b):
            step_two(l, b)
            if follow:
                step_one(l + 1, b)

        loop(4, body)

    def finish_edges(l):
        insert_edges(l)
        send(l, True)

    two_steps(0, True)
    send(0, False)
    two_steps(1, True)
    to_west.wait()
    to_east.wait()
    loop(LEV, mend_edges)
    finish_edges(0)
    send(1, False)
    finish_edges(1)

    two_steps(2, True)
    send(2, False)
    finish_edges(2)
    two_steps(3, False)
    send(3, False)
    finish_edges(3)

    order = COLS * lax.rem(me, 8)

    def ordered(row):
        row = jnp.broadcast_to(row, (8, CELLS))
        return jnp.concatenate(
            [pltpu.roll(row[:, WIDE * h:WIDE * (h + 1)], order, 1) for h in range(2)], axis=1)[0:1]

    def analyse(l):
        forward_own(l).wait()
        wait_bytes(rcv.at[l, pl.ds(0, K - MINE), :], fwd_rs.at[l])
        total = jnp.zeros((8, CELLS), F32)

        def add_rows(i, total):
            block = rcv[l, pl.ds(pl.multiple_of(i * CHUNK, CHUNK), CHUNK), :]
            return total + jnp.sum(block.reshape(CHUNK // 8, 8, CELLS), axis=0)

        total = lax.fori_loop(0, K // CHUNK, add_rows, total)
        mean = jnp.sum(total, axis=0, keepdims=True) * (1.0 / K)
        prec = ordered(cnt[l].astype(F32)) * 0.25
        weight = prec * (ordered(obs[l]) - mean) * (1.0 / (K - 1))

        def centre(i):
            at = pl.ds(pl.multiple_of(i * CHUNK, CHUNK), CHUNK)
            block = rcv[l, at, :] - mean
            pert[at, :] = block
            p0, p1, p2 = split3(block)
            ph[at, :] = p0
            pm[at, :] = p1
            pl_[at, :] = p2
            scaled = block * prec
            q0 = scaled.astype(BF16)
            qh[at, :] = q0
            ql[at, :] = (scaled - q0.astype(F32)).astype(BF16)
            drive[at, :] = jnp.sum(block * weight, axis=1, keepdims=True)

        loop(K // CHUNK, centre)

        gram = mm_t(qh[...], ph[...]) + (mm_t(qh[...], pm[...]) + mm_t(ql[...], ph[...]))
        eye = jnp.where(
            lax.broadcasted_iota(jnp.int32, (K, K), 0) == lax.broadcasted_iota(jnp.int32, (K, K), 1), 1.0, 0.0)
        system = eye + gram * (1.0 / (K - 1))
        scale = jnp.sqrt(jnp.sum(jnp.sum(system * system, axis=1, keepdims=True), axis=0, keepdims=True))
        first = system * (1.0 / scale)
        factor = 1.5 * eye - 0.5 * first
        inv[...] = factor
        root[...] = product(split3(first), split3(factor))

        def newton(i):
            held, base = split3(inv[...]), split3(root[...])
            factor = split3(1.5 * eye - 0.5 * product(held, base))
            inv[...] = product(held, factor)
            root[...] = product(base, factor)

        loop(ITERS - 2, newton)
        held, base = split3(inv[...]), split3(root[...])
        factor = split3(1.5 * eye - 0.5 * product(held, base))
        half = product(held, factor) * lax.rsqrt(scale)
        inv[...] = half

        turned = jnp.sum(half * drive[...], axis=0, keepdims=True)
        drive[...] = jnp.sum(half * turned, axis=1, keepdims=True)

        def shift(i, total):
            at = pl.ds(pl.multiple_of(i * CHUNK, CHUNK), CHUNK)
            block = pert[at, :] * drive[at, :]
            return total + jnp.sum(block.reshape(CHUNK // 8, 8, CELLS), axis=0)

        total = lax.fori_loop(0, K // CHUNK, shift, jnp.zeros((8, CELLS), F32))
        centre_row = mean + jnp.sum(total, axis=0, keepdims=True)
        h0, h1, h2 = split3(half)
        for c in range(3):
            at = slice(256 * c, 256 * (c + 1))
            cells = (ph[:, at], pm[:, at], pl_[:, at])
            ana[l, :, at] = centre_row[:, at] + product((h0, h1, h2), cells)

        backward_own(l).start()
        loop(PEERS - 1, lambda k: backward(l, k).start())

    loop(LEV, analyse)

    def finish(l):
        backward_own(l).wait()
        wait_bytes(ret.at[l, pl.ds(0, K - MINE), :], back_rs.at[l])

        def part(b):
            r, h = b // 2, lax.rem(b, 2)
            patches = [
                ret[l, pl.ds(pl.multiple_of((r * 8 + c) * MINE, MINE), MINE),
                    pl.ds(pl.multiple_of(h * WIDE, LANES), WIDE)]
                for c in range(8)
            ]
            for i, row in enumerate(sheared(patches)):
                field[l, 8 * b + i] = turned(row, -COLS * i)

        loop(4, part)


    loop(LEV, finish)

    def drain(l):
        wait_bytes(snd.at[l, pl.ds(0, PEERS - 1)], fwd_ss.at[l])
        wait_bytes(ana.at[l, pl.ds(0, K - MINE), :], back_ss.at[l])

    loop(LEV, drain)


def members_first(field, out, sem):
    def copy(m):
        return pltpu.make_async_copy(field.at[:, :, m, :], out.at[m], sem)

    loop(MINE, lambda m: copy(m).start())
    pltpu.make_async_copy(field, field, sem).wait()


def on_device(ensemble, kappa, advect, observed, counts):
    scratch = [
        pltpu.VMEM((LEV, PAD, FIELDS, WIDE), F32),
        *[pltpu.VMEM((LEV, FIELDS, LANES), F32)] * 4,
        *[pltpu.VMEM((LEV, MINE, LANES), F32)] * 2,
        pltpu.VMEM((LEV, PAD, MINE, WIDE), F32),
        pltpu.VMEM((LEV, PEERS, MINE, CELLS), F32),
        pltpu.VMEM((LEV, K, CELLS), F32),
        pltpu.VMEM((K, CELLS), F32),
        *[pltpu.VMEM((K, CELLS), BF16)] * 5,
        pltpu.VMEM((K, 1), F32),
        *[pltpu.VMEM((K, K), F32)] * 2,
        pltpu.VMEM((LEV, K, CELLS), F32),
        pltpu.VMEM((LEV, K, CELLS), F32),
        pltpu.VMEM((LEV, ROWS, MINE, WIDE), F32),
        pltpu.SemaphoreType.DMA((2,)),
        *[pltpu.SemaphoreType.DMA((2,))] * 2,
        *[pltpu.SemaphoreType.DMA((LEV,))] * 2,
        pltpu.SemaphoreType.DMA((2 * LEV,)),
        *[pltpu.SemaphoreType.DMA((LEV,))] * 2,
        pltpu.SemaphoreType.DMA((LEV,)),
    ]
    vmem = pl.BlockSpec(memory_space=pltpu.VMEM)
    whole = pl.BlockSpec(memory_space=pl.ANY)
    smem = pl.BlockSpec(memory_space=pltpu.SMEM)
    members_last = pl.pallas_call(
        kernel,
        out_shape=pltpu.VMEM((LEV, ROWS, MINE, WIDE), F32),
        in_specs=[whole, whole, smem, vmem, vmem],
        out_specs=vmem,
        scratch_shapes=scratch,
        compiler_params=pltpu.CompilerParams(
            collective_id=0, has_side_effects=True, vmem_limit_bytes=56 * 1024 * 1024),
        name="analysis",
    )(ensemble, kappa, advect, observed.reshape(LEV, 1, CELLS), counts.reshape(LEV, 1, CELLS))
    return pl.pallas_call(
        members_first,
        out_shape=jax.ShapeDtypeStruct((MINE, LEV, ROWS, WIDE), F32),
        in_specs=[whole],
        out_specs=whole,
        scratch_shapes=[pltpu.SemaphoreType.DMA],
        compiler_params=pltpu.CompilerParams(vmem_limit_bytes=1024 * 1024),
        name="members_first",
    )(members_last)


def solution(mesh):
    in_specs = (
        P("member", None, None, "tile"),
        P(None, None, "tile"),
        P(),
        P(None, "member", "tile", None),
        P(None, "member", "tile", None),
    )
    return jax.shard_map(
        on_device, mesh=mesh, in_specs=in_specs, out_specs=P("member", None, None, "tile"), check_vma=False
    )
```

```python
import jax
import jax.numpy as jnp
from jax import lax
from jax.experimental import pallas as pl
from jax.experimental.pallas import tpu as pltpu
from jax.sharding import PartitionSpec as P

MESH = pl.DeviceIdType.MESH
F32 = jnp.float32
BF16 = jnp.bfloat16
LEV = 4
ROWS = 32
PAD = ROWS + 2
WIDE = 384
CELLS = 768
COLS = 48
LANES = 128
MINE = 16
FIELDS = 24
CHUNK = 256
K = 256
PEERS = 16
TILES = 8
ITERS = 10


def loop(count, body):
    def step(i, carry):
        body(i)
        return carry

    lax.fori_loop(0, count, step, 0)


def split3(a):
    a0 = a.astype(BF16)
    rest = a - a0.astype(F32)
    a1 = rest.astype(BF16)
    return a0, a1, (rest - a1.astype(F32)).astype(BF16)


def mm(a, b):
    return jnp.dot(a, b, preferred_element_type=F32)


def mm_t(a, b):
    return lax.dot_general(a, b, (((1,), (1,)), ((), ())), preferred_element_type=F32)


def product(a, b):
    return mm(a[0], b[0]) + (
        (mm(a[0], b[1]) + mm(a[1], b[0]))
        + (mm(a[1], b[1]) + mm(a[0], b[2]) + mm(a[2], b[0]))
    )


def sheared(arrays):
    lane = lax.broadcasted_iota(jnp.int32, (MINE, LANES), 1)
    result = []
    for d in range(8):
        parts = []
        for t in range(3):
            low, high = LANES * t, LANES * (t + 1)
            first, last = low // COLS, (high - 1) // COLS
            here = [arrays[(p - d) % 8][:, low:high] for p in range(first, last + 1)]
            value = here[-1]
            for p in range(last - 1, first - 1, -1):
                value = jnp.where(lane < COLS * (p + 1) - low, here[p - first], value)
            parts.append(value)
        result.append(jnp.concatenate(parts, axis=1))
    return result


def turned(array, shift):
    shift %= array.shape[1]
    return pltpu.roll(array, shift, 1) if shift else array


def moved(here, east, west, north, south, kappa, speed):
    return here + kappa * (east + west + north + south - 4.0 * here) + speed * (west - here)


def kernel(
    ens, kap, adv, obs, cnt, field,
    ensv, head, tail, send_w, send_e, recv_e, recv_w, mend_w, mend_e, u1,
    snd, rcv, ph, pm, pl_, qh, ql, drive, inv, root, ana, ret, outv,
    in_sem, halo_ss, halo_rs, fwd_ss, fwd_rs, own_sem, back_ss, back_rs, out_sem,
):
    me = lax.axis_index("member")
    tile = lax.axis_index("tile")
    east = lax.rem(tile + 1, TILES)
    west = lax.rem(tile + TILES - 1, TILES)
    inner = pl.ds(1, ROWS)

    def load_levels(part, base, count):
        levels = pl.ds(base, count)

        def member(m):
            pltpu.make_async_copy(
                ens.at[m, levels], ensv.at[levels, inner, m, :], in_sem.at[part]).start()

        def copy_kappa(m):
            pltpu.make_async_copy(
                kap.at[levels], ensv.at[levels, inner, MINE + m, :], in_sem.at[part]).start()

        loop(MINE, member)
        loop(FIELDS - MINE, copy_kappa)

    load_levels(0, 0, 1)
    load_levels(1, 1, LEV - 1)

    barrier = pltpu.get_barrier_semaphore()

    def greet(k):
        peer = lax.rem(me + k + 1, PEERS)
        pl.semaphore_signal(barrier, inc=1, device_id={"member": peer}, device_id_type=MESH)

    loop(PEERS - 1, greet)
    for side in (east, west):
        pl.semaphore_signal(barrier, inc=1, device_id={"tile": side}, device_id_type=MESH)

    def clear(l):
        for y in (0, ROWS + 1):
            ensv[l, y] = jnp.zeros((FIELDS, WIDE), F32)
            u1[l, y] = jnp.zeros((MINE, WIDE), F32)

    loop(LEV, clear)

    def wait_bytes(ref, sem):
        pltpu.make_async_copy(ref, ref, sem).wait()

    wait_bytes(ensv.at[pl.ds(0, 1), inner], in_sem.at[0])

    def step_one(l, b):
        rows = [ensv[l, 8 * b + i, 0:MINE] for i in range(10)]
        speed = adv[l]
        for i in range(8):
            south, here, north = rows[i:i + 3]
            kappa = ensv[l, 8 * b + i + 1, MINE:FIELDS]
            kappa = jnp.concatenate([kappa, kappa], axis=0)
            u1[l, 8 * b + i + 1] = moved(here, turned(here, -1), turned(here, 1), north, south, kappa, speed)

    def step_two(l, b):
        rows = [u1[l, 8 * b + i] for i in range(10)]
        speed = adv[l]
        done = []
        for i in range(8):
            south, here, north = rows[i:i + 3]
            kappa = ensv[l, 8 * b + i + 1, MINE:FIELDS]
            kappa = jnp.concatenate([kappa, kappa], axis=0)
            row = moved(here, turned(here, -1), turned(here, 1), north, south, kappa, speed)
            done.append(turned(row, COLS * i))
        r, h = b // 2, lax.rem(b, 2)
        for c, patch in enumerate(sheared(done)):
            snd[l, r * 8 + c, :, pl.ds(pl.multiple_of(h * WIDE, LANES), WIDE)] = patch

    loop(4, lambda b: step_one(0, b))
    loop(4, lambda b: step_two(0, b))
    wait_bytes(ensv.at[pl.ds(1, LEV - 1), inner], in_sem.at[1])

    lane = lax.broadcasted_iota(jnp.int32, (FIELDS, LANES), 1)

    def edges_of(l):
        first = jnp.zeros((FIELDS, LANES), F32)
        last = jnp.zeros((FIELDS, LANES), F32)
        for y in range(ROWS):
            ends = jnp.where(lane < 64, ensv[l, y + 1, :, 0:LANES], ensv[l, y + 1, :, 2 * LANES:3 * LANES])
            ends = turned(ends, 4 * y)
            first = jnp.where(lane // 4 == y, ends, first)
            last = jnp.where(lane // 4 == (y - 1) % ROWS, ends, last)
        head[l] = first
        tail[l] = turned(last, 4)

    loop(LEV, edges_of)
    for j in range(LEV // 2):
        send_w[j] = jnp.where(lane % 4 < 2, head[2 * j], turned(head[2 * j + 1], 2))
        send_e[j] = jnp.where(lane % 4 < 2, turned(tail[2 * j + 1], -2), tail[2 * j])
    pl.semaphore_wait(barrier, PEERS + 1)

    to_west = pltpu.make_async_remote_copy(
        send_w, recv_e, halo_ss.at[0], halo_rs.at[0], device_id={"tile": west}, device_id_type=MESH)
    to_east = pltpu.make_async_remote_copy(
        send_e, recv_w, halo_ss.at[1], halo_rs.at[1], device_id={"tile": east}, device_id_type=MESH)
    to_west.start()
    to_east.start()

    def forward(l, peer):
        return pltpu.make_async_remote_copy(
            snd.at[l, peer], rcv.at[l, pl.ds(me * MINE, MINE), :], fwd_ss.at[l], fwd_rs.at[l],
            device_id={"member": peer}, device_id_type=MESH)

    def forward_own(l):
        return pltpu.make_async_copy(snd.at[l, me], rcv.at[l, pl.ds(me * MINE, MINE), :], own_sem.at[l])

    def backward(l, k):
        peer = lax.rem(me + k + 1, PEERS)
        return pltpu.make_async_remote_copy(
            ana.at[l, pl.ds(peer * MINE, MINE), :], ret.at[l, pl.ds(me * MINE, MINE), :],
            back_ss.at[l], back_rs.at[l], device_id={"member": peer}, device_id_type=MESH)

    def backward_own(l):
        at = pl.ds(me * MINE, MINE)
        return pltpu.make_async_copy(ana.at[l, at, :], ret.at[l, at, :], own_sem.at[LEV + l])

    def send(l, wanted):
        def one(k):
            peer = lax.rem(me + k, PEERS)
            column = lax.rem(peer, 8)
            outer = jnp.logical_or(column == 0, column == 7)

            @pl.when(outer if wanted else jnp.logical_not(outer))
            def _():
                @pl.when(k == 0)
                def _():
                    forward_own(l).start()

                @pl.when(k > 0)
                def _():
                    forward(l, peer).start()

        loop(PEERS, one)

    def compact(a, b, ka, kb, speed, want_a, want_b):
        place = lax.broadcasted_iota(jnp.int32, a.shape, 1)
        slot = place % 4

        def sides(x):
            south = jnp.where(place < 4, 0.0, pltpu.roll(x, 4, 1))
            north = jnp.where(place >= LANES - 4, 0.0, pltpu.roll(x, LANES - 4, 1))
            return north, south

        new_a = new_b = None
        if want_a:
            after = jnp.where(slot == 3, pltpu.roll(b, 3, 1), pltpu.roll(a, LANES - 1, 1))
            new_a = moved(a, after, pltpu.roll(a, 1, 1), *sides(a), ka, speed)
        if want_b:
            before = jnp.where(slot == 0, pltpu.roll(a, LANES - 3, 1), pltpu.roll(b, 1, 1))
            new_b = moved(b, pltpu.roll(b, LANES - 1, 1), before, *sides(b), kb, speed)
        return new_a, new_b

    def mend_edges(l):
        speed = adv[l]

        def parts(both):
            kappa = both[MINE:FIELDS]
            return both[0:MINE], jnp.concatenate([kappa, kappa], axis=0)

        from_west, from_east = recv_w[l // 2], recv_e[l // 2]
        if l % 2:
            from_west, from_east = turned(from_west, 2), turned(from_east, -2)
        (a, ka), (b, kb) = parts(from_west), parts(head[l])
        a, b = compact(a, b, ka, kb, speed, True, True)
        mend_w[l] = compact(a, b, ka, kb, speed, False, True)[1]
        (a, ka), (b, kb) = parts(tail[l]), parts(from_east)
        a, b = compact(a, b, ka, kb, speed, True, True)
        mend_e[l] = compact(a, b, ka, kb, speed, True, False)[0]

    def insert_edges(l):
        place = lax.broadcasted_iota(jnp.int32, (MINE, LANES), 1)
        for mend, c, cell in ((mend_w, 0, 0), (mend_e, 7, COLS - 2)):
            values = mend[l]
            for b in range(4):
                r, h = divmod(b, 2)
                tiles = [snd[l, r * 8 + c, :, WIDE * h + LANES * t:WIDE * h + LANES * (t + 1)] for t in range(3)]
                for i in range(8):
                    to = COLS * ((c + i) % 8) + cell
                    t, to = divmod(to, LANES)
                    source = 4 * (8 * b + i) + (2 if cell else 0)
                    value = turned(values, to - source)
                    tiles[t] = jnp.where(jnp.logical_or(place == to, place == to + 1), value, tiles[t])
                for t in range(3):
                    snd[l, r * 8 + c, :, WIDE * h + LANES * t:WIDE * h + LANES * (t + 1)] = tiles[t]

    def two_steps(l, follow):
        def body(b):
            step_two(l, b)
            if follow:
                step_one(l + 1, b)

        loop(4, body)

    def finish_edges(l):
        mend_edges(l)
        insert_edges(l)
        send(l, True)

    send(0, False)
    loop(4, lambda b: step_one(1, b))
    two_steps(1, True)
    to_west.wait()
    to_east.wait()
    finish_edges(0)
    send(1, False)
    finish_edges(1)

    two_steps(2, True)
    send(2, False)
    finish_edges(2)
    two_steps(3, False)
    send(3, False)
    finish_edges(3)

    order = COLS * lax.rem(me, 8)

    def ordered(row):
        row = jnp.broadcast_to(row, (8, CELLS))
        return jnp.concatenate(
            [pltpu.roll(row[:, WIDE * h:WIDE * (h + 1)], order, 1) for h in range(2)], axis=1)[0:1]

    def analyse(l):
        forward_own(l).wait()
        wait_bytes(rcv.at[l, pl.ds(0, K - MINE), :], fwd_rs.at[l])
        total = jnp.zeros((8, CELLS), F32)

        def add_rows(i, total):
            block = rcv[l, pl.ds(pl.multiple_of(i * CHUNK, CHUNK), CHUNK), :]
            return total + jnp.sum(block.reshape(CHUNK // 8, 8, CELLS), axis=0)

        total = lax.fori_loop(0, K // CHUNK, add_rows, total)
        mean = jnp.sum(total, axis=0, keepdims=True) * (1.0 / K)
        prec = ordered(cnt[l].astype(F32)) * 0.25
        weight = prec * (ordered(obs[l]) - mean) * (1.0 / (K - 1))

        def centre(i):
            at = pl.ds(pl.multiple_of(i * CHUNK, CHUNK), CHUNK)
            block = rcv[l, at, :] - mean
            p0, p1, p2 = split3(block)
            ph[at, :] = p0
            pm[at, :] = p1
            pl_[at, :] = p2
            scaled = block * prec
            q0 = scaled.astype(BF16)
            qh[at, :] = q0
            ql[at, :] = (scaled - q0.astype(F32)).astype(BF16)
            drive[at, :] = jnp.sum(block * weight, axis=1, keepdims=True)

        loop(K // CHUNK, centre)

        gram = mm_t(qh[...], ph[...]) + (mm_t(qh[...], pm[...]) + mm_t(ql[...], ph[...]))
        eye = jnp.where(
            lax.broadcasted_iota(jnp.int32, (K, K), 0) == lax.broadcasted_iota(jnp.int32, (K, K), 1), 1.0, 0.0)
        system = eye + gram * (1.0 / (K - 1))
        scale = jnp.sqrt(jnp.sum(jnp.sum(system * system, axis=1, keepdims=True), axis=0, keepdims=True))
        first = system * (1.0 / scale)
        factor = 1.5 * eye - 0.5 * first
        inv[...] = factor
        root[...] = product(split3(first), split3(factor))

        def newton(i):
            held, base = split3(inv[...]), split3(root[...])
            factor = split3(1.5 * eye - 0.5 * product(held, base))
            inv[...] = product(held, factor)
            root[...] = product(base, factor)

        loop(ITERS - 2, newton)
        held, base = split3(inv[...]), split3(root[...])
        factor = split3(1.5 * eye - 0.5 * product(held, base))
        half = product(held, factor) * lax.rsqrt(scale)

        once = jnp.sum(half * drive[...], axis=0, keepdims=True)
        twice = jnp.sum(half * once, axis=1, keepdims=True)
        w0, w1, w2 = split3(half + jnp.sum(eye * twice, axis=0, keepdims=True))
        for c in range(3):
            at = slice(256 * c, 256 * (c + 1))
            cells = (ph[:, at], pm[:, at], pl_[:, at])
            ana[l, :, at] = mean[:, at] + product((w0, w1, w2), cells)

        backward_own(l).start()
        loop(PEERS - 1, lambda k: backward(l, k).start())

    loop(LEV, analyse)

    def finish(l):
        backward_own(l).wait()
        wait_bytes(ret.at[l, pl.ds(0, K - MINE), :], back_rs.at[l])

        def part(b):
            r, h = b // 2, lax.rem(b, 2)
            patches = [
                ret[l, pl.ds(pl.multiple_of((r * 8 + c) * MINE, MINE), MINE),
                    pl.ds(pl.multiple_of(h * WIDE, LANES), WIDE)]
                for c in range(8)
            ]
            for i, row in enumerate(sheared(patches)):
                field[l, 8 * b + i] = turned(row, -COLS * i)

        loop(4, part)


    loop(LEV, finish)

    def drain(l):
        wait_bytes(snd.at[l, pl.ds(0, PEERS - 1)], fwd_ss.at[l])
        wait_bytes(ana.at[l, pl.ds(0, K - MINE), :], back_ss.at[l])

    loop(LEV, drain)


def members_first(field, out, sem):
    def copy(m):
        return pltpu.make_async_copy(field.at[:, :, m, :], out.at[m], sem)

    loop(MINE, lambda m: copy(m).start())
    pltpu.make_async_copy(field, field, sem).wait()


def on_device(ensemble, kappa, advect, observed, counts):
    scratch = [
        pltpu.VMEM((LEV, PAD, FIELDS, WIDE), F32),
        *[pltpu.VMEM((LEV, FIELDS, LANES), F32)] * 2,
        *[pltpu.VMEM((LEV // 2, FIELDS, LANES), F32)] * 4,
        *[pltpu.VMEM((LEV, MINE, LANES), F32)] * 2,
        pltpu.VMEM((LEV, PAD, MINE, WIDE), F32),
        pltpu.VMEM((LEV, PEERS, MINE, CELLS), F32),
        pltpu.VMEM((LEV, K, CELLS), F32),
        *[pltpu.VMEM((K, CELLS), BF16)] * 5,
        pltpu.VMEM((K, 1), F32),
        *[pltpu.VMEM((K, K), F32)] * 2,
        pltpu.VMEM((LEV, K, CELLS), F32),
        pltpu.VMEM((LEV, K, CELLS), F32),
        pltpu.VMEM((LEV, ROWS, MINE, WIDE), F32),
        pltpu.SemaphoreType.DMA((2,)),
        *[pltpu.SemaphoreType.DMA((2,))] * 2,
        *[pltpu.SemaphoreType.DMA((LEV,))] * 2,
        pltpu.SemaphoreType.DMA((2 * LEV,)),
        *[pltpu.SemaphoreType.DMA((LEV,))] * 2,
        pltpu.SemaphoreType.DMA((LEV,)),
    ]
    vmem = pl.BlockSpec(memory_space=pltpu.VMEM)
    whole = pl.BlockSpec(memory_space=pl.ANY)
    smem = pl.BlockSpec(memory_space=pltpu.SMEM)
    members_last = pl.pallas_call(
        kernel,
        out_shape=pltpu.VMEM((LEV, ROWS, MINE, WIDE), F32),
        in_specs=[whole, whole, smem, vmem, vmem],
        out_specs=vmem,
        scratch_shapes=scratch,
        compiler_params=pltpu.CompilerParams(
            collective_id=0, has_side_effects=True, vmem_limit_bytes=56 * 1024 * 1024),
        name="analysis",
    )(ensemble, kappa, advect, observed.reshape(LEV, 1, CELLS), counts.reshape(LEV, 1, CELLS))
    return pl.pallas_call(
        members_first,
        out_shape=jax.ShapeDtypeStruct((MINE, LEV, ROWS, WIDE), F32),
        in_specs=[whole],
        out_specs=whole,
        scratch_shapes=[pltpu.SemaphoreType.DMA],
        compiler_params=pltpu.CompilerParams(vmem_limit_bytes=1024 * 1024),
        name="members_first",
    )(members_last)


def solution(mesh):
    in_specs = (
        P("member", None, None, "tile"),
        P(None, None, "tile"),
        P(),
        P(None, "member", "tile", None),
        P(None, "member", "tile", None),
    )
    return jax.shard_map(
        on_device, mesh=mesh, in_specs=in_specs, out_specs=P("member", None, None, "tile"), check_vma=False
    )
```

```python
import jax
import jax.numpy as jnp
from jax import lax
from jax.experimental import pallas as pl
from jax.experimental.pallas import tpu as pltpu
from jax.sharding import PartitionSpec as P

MESH = pl.DeviceIdType.MESH
F32 = jnp.float32
BF16 = jnp.bfloat16
LEV = 4
ROWS = 32
PAD = ROWS + 2
WIDE = 384
CELLS = 768
COLS = 48
LANES = 128
MINE = 16
FIELDS = 24
CHUNK = 256
K = 256
PEERS = 16
TILES = 8
ITERS = 10


def loop(count, body):
    def step(i, carry):
        body(i)
        return carry

    lax.fori_loop(0, count, step, 0)


def split3(a):
    a0 = a.astype(BF16)
    rest = a - a0.astype(F32)
    a1 = rest.astype(BF16)
    return a0, a1, (rest - a1.astype(F32)).astype(BF16)


def mm(a, b):
    return jnp.dot(a, b, preferred_element_type=F32)


def mm_t(a, b):
    return lax.dot_general(a, b, (((1,), (1,)), ((), ())), preferred_element_type=F32)


def product(a, b):
    return mm(a[0], b[0]) + (
        (mm(a[0], b[1]) + mm(a[1], b[0]))
        + (mm(a[1], b[1]) + mm(a[0], b[2]) + mm(a[2], b[0]))
    )


def sheared(arrays):
    lane = lax.broadcasted_iota(jnp.int32, (MINE, LANES), 1)
    result = []
    for d in range(8):
        parts = []
        for t in range(3):
            low, high = LANES * t, LANES * (t + 1)
            first, last = low // COLS, (high - 1) // COLS
            here = [arrays[(p - d) % 8][:, low:high] for p in range(first, last + 1)]
            value = here[-1]
            for p in range(last - 1, first - 1, -1):
                value = jnp.where(lane < COLS * (p + 1) - low, here[p - first], value)
            parts.append(value)
        result.append(jnp.concatenate(parts, axis=1))
    return result


def turned(array, shift):
    shift %= array.shape[1]
    return pltpu.roll(array, shift, 1) if shift else array


def moved(here, east, west, north, south, kappa, speed):
    return here + kappa * (east + west + north + south - 4.0 * here) + speed * (west - here)


def kernel(
    ens, kap, adv, obs, cnt, field,
    ensv, kapv, head, tail, send_w, send_e, recv_e, recv_w, mend_w, mend_e, u1,
    snd, rcv, ph, pm, pl_, qh, ql, drive, inv, root, ana, ret, outv,
    in_sem, halo_ss, halo_rs, fwd_ss, fwd_rs, own_sem, back_ss, back_rs, out_sem,
):
    me = lax.axis_index("member")
    tile = lax.axis_index("tile")
    east = lax.rem(tile + 1, TILES)
    west = lax.rem(tile + TILES - 1, TILES)
    inner = pl.ds(1, ROWS)

    def load_levels(part, base, count):
        levels = pl.ds(base, count)

        def member(m):
            pltpu.make_async_copy(
                ens.at[m, levels], ensv.at[levels, inner, m, :], in_sem.at[part]).start()

        loop(MINE, member)

    barrier = pltpu.get_barrier_semaphore()

    def greet(k):
        peer = lax.rem(me + k + 1, PEERS)
        pl.semaphore_signal(barrier, inc=1, device_id={"member": peer}, device_id_type=MESH)

    loop(PEERS - 1, greet)
    for side in (east, west):
        pl.semaphore_signal(barrier, inc=1, device_id={"tile": side}, device_id_type=MESH)

    load_kappa = pltpu.make_async_copy(kap, kapv, in_sem.at[2])
    load_kappa.start()
    load_levels(0, 0, 1)

    load_levels(1, 1, LEV - 1)

    def clear(l):
        for y in (0, ROWS + 1):
            ensv[l, y] = jnp.zeros((FIELDS, WIDE), F32)
            u1[l, y] = jnp.zeros((MINE, WIDE), F32)

    loop(LEV, clear)

    def wait_bytes(ref, sem):
        pltpu.make_async_copy(ref, ref, sem).wait()

    def spread_kappa(j):
        l, b = j // 4, lax.rem(j, 4)
        rows = kapv[l, pl.ds(pl.multiple_of(8 * b, 8), 8), :]
        for i in range(8):
            ensv[l, 8 * b + i + 1, MINE:FIELDS] = jnp.broadcast_to(rows[i:i + 1], (FIELDS - MINE, WIDE))

    load_kappa.wait()
    loop(4, spread_kappa)
    wait_bytes(ensv.at[pl.ds(0, 1), inner, 0:MINE], in_sem.at[0])

    def advanced(source, count, l, r):
        rows = [source[l, 16 * r + i, 0:count] for i in range(18)]
        speed = adv[l]
        result = []
        for i in range(16):
            south, here, north = rows[i:i + 3]
            kappa = ensv[l, 16 * r + i + 1, MINE:FIELDS]
            kappa = jnp.concatenate([kappa, kappa], axis=0)
            result.append(moved(here, turned(here, -1), turned(here, 1), north, south, kappa, speed))
        return result

    def step_one(l, r):
        for i, row in enumerate(advanced(ensv, MINE, l, r)):
            u1[l, 16 * r + i + 1] = row

    def step_two(l, r):
        rows = advanced(u1, MINE, l, r)
        for h in range(2):
            done = [turned(rows[8 * h + i], COLS * i) for i in range(8)]
            for c, patch in enumerate(sheared(done)):
                snd[l, r * 8 + c, :, WIDE * h:WIDE * (h + 1)] = patch

    loop(2, lambda r: step_one(0, r))
    loop(2, lambda r: step_two(0, r))
    loop(4 * LEV - 4, lambda j: spread_kappa(j + 4))
    wait_bytes(ensv.at[pl.ds(1, LEV - 1), inner, 0:MINE], in_sem.at[1])

    lane = lax.broadcasted_iota(jnp.int32, (FIELDS, LANES), 1)

    def edges_of(l):
        first = jnp.zeros((FIELDS, LANES), F32)
        last = jnp.zeros((FIELDS, LANES), F32)
        for y in range(ROWS):
            ends = jnp.where(lane < 64, ensv[l, y + 1, :, 0:LANES], ensv[l, y + 1, :, 2 * LANES:3 * LANES])
            ends = turned(ends, 4 * y)
            first = jnp.where(lane // 4 == y, ends, first)
            last = jnp.where(lane // 4 == (y - 1) % ROWS, ends, last)
        head[l] = first
        tail[l] = turned(last, 4)

    loop(LEV, edges_of)
    for j in range(LEV // 2):
        send_w[j] = jnp.where(lane % 4 < 2, head[2 * j], turned(head[2 * j + 1], 2))
        send_e[j] = jnp.where(lane % 4 < 2, turned(tail[2 * j + 1], -2), tail[2 * j])
    pl.semaphore_wait(barrier, PEERS + 1)

    to_west = pltpu.make_async_remote_copy(
        send_w, recv_e, halo_ss.at[0], halo_rs.at[0], device_id={"tile": west}, device_id_type=MESH)
    to_east = pltpu.make_async_remote_copy(
        send_e, recv_w, halo_ss.at[1], halo_rs.at[1], device_id={"tile": east}, device_id_type=MESH)
    to_west.start()
    to_east.start()

    def forward(l, peer):
        return pltpu.make_async_remote_copy(
            snd.at[l, peer], rcv.at[l, pl.ds(me * MINE, MINE), :], fwd_ss.at[l], fwd_rs.at[l],
            device_id={"member": peer}, device_id_type=MESH)

    def forward_own(l):
        return pltpu.make_async_copy(snd.at[l, me], rcv.at[l, pl.ds(me * MINE, MINE), :], own_sem.at[l])

    def backward(l, k):
        peer = lax.rem(me + k + 1, PEERS)
        return pltpu.make_async_remote_copy(
            ana.at[l, pl.ds(peer * MINE, MINE), :], ret.at[l, pl.ds(me * MINE, MINE), :],
            back_ss.at[l], back_rs.at[l], device_id={"member": peer}, device_id_type=MESH)

    def backward_own(l):
        at = pl.ds(me * MINE, MINE)
        return pltpu.make_async_copy(ana.at[l, at, :], ret.at[l, at, :], own_sem.at[LEV + l])

    def send(l, wanted):
        def one(k):
            peer = lax.rem(me + k, PEERS)
            column = lax.rem(peer, 8)
            outer = jnp.logical_or(column == 0, column == 7)

            @pl.when(outer if wanted else jnp.logical_not(outer))
            def _():
                @pl.when(k == 0)
                def _():
                    forward_own(l).start()

                @pl.when(k > 0)
                def _():
                    forward(l, peer).start()

        loop(PEERS, one)

    def compact(a, b, ka, kb, speed, want_a, want_b):
        place = lax.broadcasted_iota(jnp.int32, a.shape, 1)
        slot = place % 4

        def sides(x):
            south = jnp.where(place < 4, 0.0, pltpu.roll(x, 4, 1))
            north = jnp.where(place >= LANES - 4, 0.0, pltpu.roll(x, LANES - 4, 1))
            return north, south

        new_a = new_b = None
        if want_a:
            after = jnp.where(slot == 3, pltpu.roll(b, 3, 1), pltpu.roll(a, LANES - 1, 1))
            new_a = moved(a, after, pltpu.roll(a, 1, 1), *sides(a), ka, speed)
        if want_b:
            before = jnp.where(slot == 0, pltpu.roll(a, LANES - 3, 1), pltpu.roll(b, 1, 1))
            new_b = moved(b, pltpu.roll(b, LANES - 1, 1), before, *sides(b), kb, speed)
        return new_a, new_b

    def mend_edges(l):
        speed = adv[l]

        def parts(both):
            kappa = both[MINE:FIELDS]
            return both[0:MINE], jnp.concatenate([kappa, kappa], axis=0)

        from_west, from_east = recv_w[l // 2], recv_e[l // 2]
        if l % 2:
            from_west, from_east = turned(from_west, 2), turned(from_east, -2)
        (a, ka), (b, kb) = parts(from_west), parts(head[l])
        a, b = compact(a, b, ka, kb, speed, True, True)
        mend_w[l] = compact(a, b, ka, kb, speed, False, True)[1]
        (a, ka), (b, kb) = parts(tail[l]), parts(from_east)
        a, b = compact(a, b, ka, kb, speed, True, True)
        mend_e[l] = compact(a, b, ka, kb, speed, True, False)[0]

    def insert_edges(l):
        place = lax.broadcasted_iota(jnp.int32, (MINE, LANES), 1)
        for mend, c, cell in ((mend_w, 0, 0), (mend_e, 7, COLS - 2)):
            values = mend[l]
            for b in range(4):
                r, h = divmod(b, 2)
                tiles = [snd[l, r * 8 + c, :, WIDE * h + LANES * t:WIDE * h + LANES * (t + 1)] for t in range(3)]
                for i in range(8):
                    to = COLS * ((c + i) % 8) + cell
                    t, to = divmod(to, LANES)
                    source = 4 * (8 * b + i) + (2 if cell else 0)
                    value = turned(values, to - source)
                    tiles[t] = jnp.where(jnp.logical_or(place == to, place == to + 1), value, tiles[t])
                for t in range(3):
                    snd[l, r * 8 + c, :, WIDE * h + LANES * t:WIDE * h + LANES * (t + 1)] = tiles[t]

    def two_steps(l, follow):
        def body(r):
            step_two(l, r)
            if follow:
                step_one(l + 1, r)

        loop(2, body)

    def finish_edges(l):
        mend_edges(l)
        insert_edges(l)
        send(l, True)

    send(0, False)
    loop(2, lambda r: step_one(1, r))
    two_steps(1, True)
    send(1, False)
    two_steps(2, True)
    to_west.wait()
    to_east.wait()
    finish_edges(0)
    finish_edges(1)
    send(2, False)
    finish_edges(2)
    two_steps(3, False)
    send(3, False)
    finish_edges(3)

    order = COLS * lax.rem(me, 8)

    def ordered(row):
        row = jnp.broadcast_to(row, (8, CELLS))
        return jnp.concatenate(
            [pltpu.roll(row[:, WIDE * h:WIDE * (h + 1)], order, 1) for h in range(2)], axis=1)[0:1]

    def analyse(l):
        forward_own(l).wait()
        wait_bytes(rcv.at[l, pl.ds(0, K - MINE), :], fwd_rs.at[l])
        total = jnp.zeros((8, CELLS), F32)

        def add_rows(i, total):
            block = rcv[l, pl.ds(pl.multiple_of(i * CHUNK, CHUNK), CHUNK), :]
            return total + jnp.sum(block.reshape(CHUNK // 8, 8, CELLS), axis=0)

        total = lax.fori_loop(0, K // CHUNK, add_rows, total)
        mean = jnp.sum(total, axis=0, keepdims=True) * (1.0 / K)
        prec = ordered(cnt[l].astype(F32)) * 0.25
        weight = prec * (ordered(obs[l]) - mean) * (1.0 / (K - 1))

        def centre(i):
            at = pl.ds(pl.multiple_of(i * CHUNK, CHUNK), CHUNK)
            block = rcv[l, at, :] - mean
            p0, p1, p2 = split3(block)
            ph[at, :] = p0
            pm[at, :] = p1
            pl_[at, :] = p2
            scaled = block * prec
            q0 = scaled.astype(BF16)
            qh[at, :] = q0
            ql[at, :] = (scaled - q0.astype(F32)).astype(BF16)
            drive[at, :] = jnp.sum(block * weight, axis=1, keepdims=True)

        loop(K // CHUNK, centre)

        gram = mm_t(qh[...], ph[...]) + (mm_t(qh[...], pm[...]) + mm_t(ql[...], ph[...]))
        eye = jnp.where(
            lax.broadcasted_iota(jnp.int32, (K, K), 0) == lax.broadcasted_iota(jnp.int32, (K, K), 1), 1.0, 0.0)
        system = eye + gram * (1.0 / (K - 1))
        scale = jnp.sqrt(jnp.sum(jnp.sum(system * system, axis=1, keepdims=True), axis=0, keepdims=True))
        first = system * (1.0 / scale)
        factor = 1.5 * eye - 0.5 * first
        inv[...] = factor
        root[...] = product(split3(first), split3(factor))

        def newton(i):
            held, base = split3(inv[...]), split3(root[...])
            factor = split3(1.5 * eye - 0.5 * product(held, base))
            inv[...] = product(held, factor)
            root[...] = product(base, factor)

        loop(ITERS - 2, newton)
        held, base = split3(inv[...]), split3(root[...])
        factor = split3(1.5 * eye - 0.5 * product(held, base))
        half = product(held, factor) * lax.rsqrt(scale)

        once = jnp.sum(half * drive[...], axis=0, keepdims=True)
        twice = jnp.sum(half * once, axis=1, keepdims=True)
        w0, w1, w2 = split3(half + jnp.sum(eye * twice, axis=0, keepdims=True))
        for c in range(3):
            at = slice(256 * c, 256 * (c + 1))
            cells = (ph[:, at], pm[:, at], pl_[:, at])
            ana[l, :, at] = mean[:, at] + product((w0, w1, w2), cells)

        backward_own(l).start()
        loop(PEERS - 1, lambda k: backward(l, k).start())

    loop(LEV, analyse)

    def finish(l):
        backward_own(l).wait()
        wait_bytes(ret.at[l, pl.ds(0, K - MINE), :], back_rs.at[l])

        def part(r):
            for h in range(2):
                patches = [
                    ret[l, pl.ds(pl.multiple_of((r * 8 + c) * MINE, MINE), MINE), WIDE * h:WIDE * (h + 1)]
                    for c in range(8)
                ]
                for i, row in enumerate(sheared(patches)):
                    field[l, 16 * r + 8 * h + i] = turned(row, -COLS * i)

        loop(2, part)


    loop(LEV, finish)

    def drain(l):
        wait_bytes(snd.at[l, pl.ds(0, PEERS - 1)], fwd_ss.at[l])
        wait_bytes(ana.at[l, pl.ds(0, K - MINE), :], back_ss.at[l])

    loop(LEV, drain)


def members_first(field, out, sem):
    def copy(m):
        return pltpu.make_async_copy(field.at[:, :, m, :], out.at[m], sem)

    loop(MINE, lambda m: copy(m).start())
    pltpu.make_async_copy(field, field, sem).wait()


def on_device(ensemble, kappa, advect, observed, counts):
    scratch = [
        pltpu.VMEM((LEV, PAD, FIELDS, WIDE), F32),
        pltpu.VMEM((LEV, ROWS, WIDE), F32),
        *[pltpu.VMEM((LEV, FIELDS, LANES), F32)] * 2,
        *[pltpu.VMEM((LEV // 2, FIELDS, LANES), F32)] * 4,
        *[pltpu.VMEM((LEV, MINE, LANES), F32)] * 2,
        pltpu.VMEM((LEV, PAD, MINE, WIDE), F32),
        pltpu.VMEM((LEV, PEERS, MINE, CELLS), F32),
        pltpu.VMEM((LEV, K, CELLS), F32),
        *[pltpu.VMEM((K, CELLS), BF16)] * 5,
        pltpu.VMEM((K, 1), F32),
        *[pltpu.VMEM((K, K), F32)] * 2,
        pltpu.VMEM((LEV, K, CELLS), F32),
        pltpu.VMEM((LEV, K, CELLS), F32),
        pltpu.VMEM((LEV, ROWS, MINE, WIDE), F32),
        pltpu.SemaphoreType.DMA((3,)),
        *[pltpu.SemaphoreType.DMA((2,))] * 2,
        *[pltpu.SemaphoreType.DMA((LEV,))] * 2,
        pltpu.SemaphoreType.DMA((2 * LEV,)),
        *[pltpu.SemaphoreType.DMA((LEV,))] * 2,
        pltpu.SemaphoreType.DMA((LEV,)),
    ]
    vmem = pl.BlockSpec(memory_space=pltpu.VMEM)
    whole = pl.BlockSpec(memory_space=pl.ANY)
    smem = pl.BlockSpec(memory_space=pltpu.SMEM)
    members_last = pl.pallas_call(
        kernel,
        out_shape=pltpu.VMEM((LEV, ROWS, MINE, WIDE), F32),
        in_specs=[whole, whole, smem, vmem, vmem],
        out_specs=vmem,
        scratch_shapes=scratch,
        compiler_params=pltpu.CompilerParams(
            collective_id=0, has_side_effects=True, vmem_limit_bytes=56 * 1024 * 1024),
        name="analysis",
    )(ensemble, kappa, advect, observed.reshape(LEV, 1, CELLS), counts.reshape(LEV, 1, CELLS))
    return pl.pallas_call(
        members_first,
        out_shape=jax.ShapeDtypeStruct((MINE, LEV, ROWS, WIDE), F32),
        in_specs=[whole],
        out_specs=whole,
        scratch_shapes=[pltpu.SemaphoreType.DMA],
        compiler_params=pltpu.CompilerParams(vmem_limit_bytes=1024 * 1024),
        name="members_first",
    )(members_last)


def solution(mesh):
    in_specs = (
        P("member", None, None, "tile"),
        P(None, None, "tile"),
        P(),
        P(None, "member", "tile", None),
        P(None, "member", "tile", None),
    )
    return jax.shard_map(
        on_device, mesh=mesh, in_specs=in_specs, out_specs=P("member", None, None, "tile"), check_vma=False
    )
```

```python
import jax
import jax.numpy as jnp
from jax import lax
from jax.experimental import pallas as pl
from jax.experimental.pallas import tpu as pltpu
from jax.sharding import PartitionSpec as P

MESH = pl.DeviceIdType.MESH
F32 = jnp.float32
BF16 = jnp.bfloat16
LEV = 4
ROWS = 32
PAD = ROWS + 2
WIDE = 384
CELLS = 768
COLS = 48
LANES = 128
MINE = 16
FIELDS = 24
CHUNK = 256
K = 256
PEERS = 16
TILES = 8
ITERS = 10


def loop(count, body):
    def step(i, carry):
        body(i)
        return carry

    lax.fori_loop(0, count, step, 0)


def split3(a):
    a0 = a.astype(BF16)
    rest = a - a0.astype(F32)
    a1 = rest.astype(BF16)
    return a0, a1, (rest - a1.astype(F32)).astype(BF16)


def mm(a, b):
    return jnp.dot(a, b, preferred_element_type=F32)


def mm_t(a, b):
    return lax.dot_general(a, b, (((1,), (1,)), ((), ())), preferred_element_type=F32)


def product(a, b):
    return mm(a[0], b[0]) + (
        (mm(a[0], b[1]) + mm(a[1], b[0]))
        + (mm(a[1], b[1]) + mm(a[0], b[2]) + mm(a[2], b[0]))
    )


def sheared(arrays):
    lane = lax.broadcasted_iota(jnp.int32, (MINE, LANES), 1)
    result = []
    for d in range(8):
        parts = []
        for t in range(3):
            low, high = LANES * t, LANES * (t + 1)
            first, last = low // COLS, (high - 1) // COLS
            here = [arrays[(p - d) % 8][:, low:high] for p in range(first, last + 1)]
            value = here[-1]
            for p in range(last - 1, first - 1, -1):
                value = jnp.where(lane < COLS * (p + 1) - low, here[p - first], value)
            parts.append(value)
        result.append(jnp.concatenate(parts, axis=1))
    return result


def turned(array, shift):
    shift %= array.shape[1]
    return pltpu.roll(array, shift, 1) if shift else array


def moved(here, east, west, north, south, kappa, speed):
    return here + kappa * (east + west + north + south - 4.0 * here) + speed * (west - here)


def unpack(patches_ref, rows_ref, r):
    for h in range(2):
        patches = [
            patches_ref[pl.ds(pl.multiple_of((r * 8 + c) * MINE, MINE), MINE), WIDE * h:WIDE * (h + 1)]
            for c in range(8)
        ]
        for i, row in enumerate(sheared(patches)):
            rows_ref[16 * r + 8 * h + i] = turned(row, -COLS * i)


def kernel(
    ens, kap, adv, obs, cnt, field, last,
    ensv, kapv, head, tail, send_w, send_e, recv_e, recv_w, mend_w, mend_e, u1,
    snd, rcv, ph, pm, pl_, qh, ql, drive, inv, root, ana, ret,
    in_sem, halo_ss, halo_rs, fwd_ss, fwd_rs, own_sem, back_ss, back_rs,
):
    me = lax.axis_index("member")
    tile = lax.axis_index("tile")
    east = lax.rem(tile + 1, TILES)
    west = lax.rem(tile + TILES - 1, TILES)
    inner = pl.ds(1, ROWS)

    def load_levels(part, base, count):
        levels = pl.ds(base, count)

        def member(m):
            pltpu.make_async_copy(
                ens.at[m, levels], ensv.at[levels, inner, m, :], in_sem.at[part]).start()

        loop(MINE, member)

    barrier = pltpu.get_barrier_semaphore()

    def greet(k):
        peer = lax.rem(me + k + 1, PEERS)
        pl.semaphore_signal(barrier, inc=1, device_id={"member": peer}, device_id_type=MESH)

    loop(PEERS - 1, greet)
    for side in (east, west):
        pl.semaphore_signal(barrier, inc=1, device_id={"tile": side}, device_id_type=MESH)

    load_kappa = pltpu.make_async_copy(kap, kapv, in_sem.at[2])
    load_kappa.start()
    load_levels(0, 0, 1)

    load_levels(1, 1, LEV - 1)

    def clear(l):
        for y in (0, ROWS + 1):
            ensv[l, y] = jnp.zeros((FIELDS, WIDE), F32)
            u1[l, y] = jnp.zeros((MINE, WIDE), F32)

    loop(LEV, clear)

    def wait_bytes(ref, sem):
        pltpu.make_async_copy(ref, ref, sem).wait()

    def spread_kappa(j):
        l, b = j // 4, lax.rem(j, 4)
        rows = kapv[l, pl.ds(pl.multiple_of(8 * b, 8), 8), :]
        for i in range(8):
            ensv[l, 8 * b + i + 1, MINE:FIELDS] = jnp.broadcast_to(rows[i:i + 1], (FIELDS - MINE, WIDE))

    load_kappa.wait()
    loop(4, spread_kappa)
    wait_bytes(ensv.at[pl.ds(0, 1), inner, 0:MINE], in_sem.at[0])

    def advanced(source, count, l, r):
        rows = [source[l, 16 * r + i, 0:count] for i in range(18)]
        speed = adv[l]
        result = []
        for i in range(16):
            south, here, north = rows[i:i + 3]
            kappa = ensv[l, 16 * r + i + 1, MINE:FIELDS]
            kappa = jnp.concatenate([kappa, kappa], axis=0)
            result.append(moved(here, turned(here, -1), turned(here, 1), north, south, kappa, speed))
        return result

    def step_one(l, r):
        for i, row in enumerate(advanced(ensv, MINE, l, r)):
            u1[l, 16 * r + i + 1] = row

    def step_two(l, r):
        rows = advanced(u1, MINE, l, r)
        for h in range(2):
            done = [turned(rows[8 * h + i], COLS * i) for i in range(8)]
            for c, patch in enumerate(sheared(done)):
                snd[l, r * 8 + c, :, WIDE * h:WIDE * (h + 1)] = patch

    loop(2, lambda r: step_one(0, r))
    loop(2, lambda r: step_two(0, r))
    loop(4 * LEV - 4, lambda j: spread_kappa(j + 4))
    wait_bytes(ensv.at[pl.ds(1, LEV - 1), inner, 0:MINE], in_sem.at[1])

    lane = lax.broadcasted_iota(jnp.int32, (FIELDS, LANES), 1)

    def edges_of(j):
        for l in (2 * j, 2 * j + 1):
            first = jnp.zeros((FIELDS, LANES), F32)
            last = jnp.zeros((FIELDS, LANES), F32)
            for y in range(ROWS):
                ends = jnp.where(lane < 64, ensv[l, y + 1, :, 0:LANES], ensv[l, y + 1, :, 2 * LANES:3 * LANES])
                ends = turned(ends, 4 * y)
                first = jnp.where(lane // 4 == y, ends, first)
                last = jnp.where(lane // 4 == (y - 1) % ROWS, ends, last)
            head[l] = first
            tail[l] = turned(last, 4)

    loop(LEV // 2, edges_of)
    for j in range(LEV // 2):
        send_w[j] = jnp.where(lane % 4 < 2, head[2 * j], turned(head[2 * j + 1], 2))
        send_e[j] = jnp.where(lane % 4 < 2, turned(tail[2 * j + 1], -2), tail[2 * j])
    pl.semaphore_wait(barrier, PEERS + 1)

    to_west = pltpu.make_async_remote_copy(
        send_w, recv_e, halo_ss.at[0], halo_rs.at[0], device_id={"tile": west}, device_id_type=MESH)
    to_east = pltpu.make_async_remote_copy(
        send_e, recv_w, halo_ss.at[1], halo_rs.at[1], device_id={"tile": east}, device_id_type=MESH)
    to_west.start()
    to_east.start()

    def forward(l, peer):
        return pltpu.make_async_remote_copy(
            snd.at[l, peer], rcv.at[l, pl.ds(me * MINE, MINE), :], fwd_ss.at[l], fwd_rs.at[l],
            device_id={"member": peer}, device_id_type=MESH)

    def forward_own(l):
        return pltpu.make_async_copy(snd.at[l, me], rcv.at[l, pl.ds(me * MINE, MINE), :], own_sem.at[l])

    def send_back(l, target):
        mine = pl.ds(me * MINE, MINE)
        pltpu.make_async_copy(ana.at[l, mine, :], target.at[mine, :], own_sem.at[LEV + l]).start()

        def one(k):
            peer = lax.rem(me + k + 1, PEERS)
            pltpu.make_async_remote_copy(
                ana.at[l, pl.ds(peer * MINE, MINE), :], target.at[mine, :], back_ss.at[l], back_rs.at[l],
                device_id={"member": peer}, device_id_type=MESH).start()

        loop(PEERS - 1, one)

    def wait_back(l, target):
        wait_bytes(target.at[pl.ds(0, MINE), :], own_sem.at[LEV + l])
        wait_bytes(target.at[pl.ds(0, K - MINE), :], back_rs.at[l])

    def send(l, wanted):
        def one(k):
            peer = lax.rem(me + k, PEERS)
            column = lax.rem(peer, 8)
            outer = jnp.logical_or(column == 0, column == 7)

            @pl.when(outer if wanted else jnp.logical_not(outer))
            def _():
                @pl.when(k == 0)
                def _():
                    forward_own(l).start()

                @pl.when(k > 0)
                def _():
                    forward(l, peer).start()

        loop(PEERS, one)

    def compact(a, b, ka, kb, speed, want_a, want_b):
        place = lax.broadcasted_iota(jnp.int32, a.shape, 1)
        slot = place % 4

        def sides(x):
            south = jnp.where(place < 4, 0.0, pltpu.roll(x, 4, 1))
            north = jnp.where(place >= LANES - 4, 0.0, pltpu.roll(x, LANES - 4, 1))
            return north, south

        new_a = new_b = None
        if want_a:
            after = jnp.where(slot == 3, pltpu.roll(b, 3, 1), pltpu.roll(a, LANES - 1, 1))
            new_a = moved(a, after, pltpu.roll(a, 1, 1), *sides(a), ka, speed)
        if want_b:
            before = jnp.where(slot == 0, pltpu.roll(a, LANES - 3, 1), pltpu.roll(b, 1, 1))
            new_b = moved(b, pltpu.roll(b, LANES - 1, 1), before, *sides(b), kb, speed)
        return new_a, new_b

    def mend_edges(l):
        speed = adv[l]

        def parts(both):
            kappa = both[MINE:FIELDS]
            return both[0:MINE], jnp.concatenate([kappa, kappa], axis=0)

        from_west, from_east = recv_w[l // 2], recv_e[l // 2]
        if l % 2:
            from_west, from_east = turned(from_west, 2), turned(from_east, -2)
        (a, ka), (b, kb) = parts(from_west), parts(head[l])
        a, b = compact(a, b, ka, kb, speed, True, True)
        mend_w[l] = compact(a, b, ka, kb, speed, False, True)[1]
        (a, ka), (b, kb) = parts(tail[l]), parts(from_east)
        a, b = compact(a, b, ka, kb, speed, True, True)
        mend_e[l] = compact(a, b, ka, kb, speed, True, False)[0]

    def insert_edges(l):
        place = lax.broadcasted_iota(jnp.int32, (MINE, LANES), 1)
        for mend, c, cell in ((mend_w, 0, 0), (mend_e, 7, COLS - 2)):
            values = mend[l]
            for b in range(4):
                r, h = divmod(b, 2)
                tiles = [snd[l, r * 8 + c, :, WIDE * h + LANES * t:WIDE * h + LANES * (t + 1)] for t in range(3)]
                for i in range(8):
                    to = COLS * ((c + i) % 8) + cell
                    t, to = divmod(to, LANES)
                    source = 4 * (8 * b + i) + (2 if cell else 0)
                    value = turned(values, to - source)
                    tiles[t] = jnp.where(jnp.logical_or(place == to, place == to + 1), value, tiles[t])
                for t in range(3):
                    snd[l, r * 8 + c, :, WIDE * h + LANES * t:WIDE * h + LANES * (t + 1)] = tiles[t]

    def two_steps(l, follow):
        def body(r):
            step_two(l, r)
            if follow:
                step_one(l + 1, r)

        loop(2, body)

    def finish_edges(l):
        mend_edges(l)
        insert_edges(l)
        send(l, True)

    send(0, False)
    loop(2, lambda r: step_one(1, r))
    two_steps(1, True)
    send(1, False)
    two_steps(2, True)
    to_west.wait()
    to_east.wait()
    finish_edges(0)
    finish_edges(1)
    send(2, False)
    finish_edges(2)
    two_steps(3, False)
    send(3, False)
    finish_edges(3)

    order = COLS * lax.rem(me, 8)

    def ordered(row):
        row = jnp.broadcast_to(row, (8, CELLS))
        return jnp.concatenate(
            [pltpu.roll(row[:, WIDE * h:WIDE * (h + 1)], order, 1) for h in range(2)], axis=1)[0:1]

    def analyse(l):
        forward_own(l).wait()
        wait_bytes(rcv.at[l, pl.ds(0, K - MINE), :], fwd_rs.at[l])
        total = jnp.zeros((8, CELLS), F32)

        def add_rows(i, total):
            block = rcv[l, pl.ds(pl.multiple_of(i * CHUNK, CHUNK), CHUNK), :]
            return total + jnp.sum(block.reshape(CHUNK // 8, 8, CELLS), axis=0)

        total = lax.fori_loop(0, K // CHUNK, add_rows, total)
        mean = jnp.sum(total, axis=0, keepdims=True) * (1.0 / K)
        prec = ordered(cnt[l].astype(F32)) * 0.25
        weight = prec * (ordered(obs[l]) - mean) * (1.0 / (K - 1))

        def centre(i):
            at = pl.ds(pl.multiple_of(i * CHUNK, CHUNK), CHUNK)
            block = rcv[l, at, :] - mean
            p0, p1, p2 = split3(block)
            ph[at, :] = p0
            pm[at, :] = p1
            pl_[at, :] = p2
            scaled = block * prec
            q0 = scaled.astype(BF16)
            qh[at, :] = q0
            ql[at, :] = (scaled - q0.astype(F32)).astype(BF16)
            drive[at, :] = jnp.sum(block * weight, axis=1, keepdims=True)

        loop(K // CHUNK, centre)

        gram = mm_t(qh[...], ph[...]) + (mm_t(qh[...], pm[...]) + mm_t(ql[...], ph[...]))
        eye = jnp.where(
            lax.broadcasted_iota(jnp.int32, (K, K), 0) == lax.broadcasted_iota(jnp.int32, (K, K), 1), 1.0, 0.0)
        system = eye + gram * (1.0 / (K - 1))
        scale = jnp.sqrt(jnp.sum(jnp.sum(system * system, axis=1, keepdims=True), axis=0, keepdims=True))
        first = system * (1.0 / scale)
        factor = 1.5 * eye - 0.5 * first
        inv[...] = factor
        root[...] = product(split3(first), split3(factor))

        def newton(i):
            held, base = split3(inv[...]), split3(root[...])
            factor = split3(1.5 * eye - 0.5 * product(held, base))
            inv[...] = product(held, factor)
            root[...] = product(base, factor)

        loop(ITERS - 2, newton)
        held, base = split3(inv[...]), split3(root[...])
        factor = split3(1.5 * eye - 0.5 * product(held, base))
        half = product(held, factor) * lax.rsqrt(scale)

        once = jnp.sum(half * drive[...], axis=0, keepdims=True)
        twice = jnp.sum(half * once, axis=1, keepdims=True)
        w0, w1, w2 = split3(half + jnp.sum(eye * twice, axis=0, keepdims=True))
        for c in range(3):
            at = slice(256 * c, 256 * (c + 1))
            cells = (ph[:, at], pm[:, at], pl_[:, at])
            ana[l, :, at] = mean[:, at] + product((w0, w1, w2), cells)

        @pl.when(l < LEV - 1)
        def _():
            send_back(l, ret.at[l])

        @pl.when(l == LEV - 1)
        def _():
            send_back(l, last)

    loop(LEV, analyse)

    def drain(l):
        wait_bytes(snd.at[l, pl.ds(0, PEERS - 1)], fwd_ss.at[l])
        wait_bytes(ana.at[l, pl.ds(0, K - MINE), :], back_ss.at[l])

    def finish(l):
        wait_back(l, ret.at[l])
        loop(2, lambda r: unpack(ret.at[l], field.at[l], r))
        drain(l)

    loop(LEV - 1, finish)
    drain(LEV - 1)
    wait_back(LEV - 1, last)


def members_first(field, last, out, spare, sems):
    early = pl.ds(0, LEV - 1)
    loop(MINE, lambda m: pltpu.make_async_copy(field.at[:, :, m, :], out.at[m, early], sems.at[0]).start())
    loop(2, lambda r: unpack(last, spare, r))
    loop(MINE, lambda m: pltpu.make_async_copy(spare.at[:, m, :], out.at[m, LEV - 1], sems.at[1]).start())
    pltpu.make_async_copy(field, field, sems.at[0]).wait()
    pltpu.make_async_copy(spare, spare, sems.at[1]).wait()


def on_device(ensemble, kappa, advect, observed, counts):
    scratch = [
        pltpu.VMEM((LEV, PAD, FIELDS, WIDE), F32),
        pltpu.VMEM((LEV, ROWS, WIDE), F32),
        *[pltpu.VMEM((LEV, FIELDS, LANES), F32)] * 2,
        *[pltpu.VMEM((LEV // 2, FIELDS, LANES), F32)] * 4,
        *[pltpu.VMEM((LEV, MINE, LANES), F32)] * 2,
        pltpu.VMEM((LEV, PAD, MINE, WIDE), F32),
        pltpu.VMEM((LEV, PEERS, MINE, CELLS), F32),
        pltpu.VMEM((LEV, K, CELLS), F32),
        *[pltpu.VMEM((K, CELLS), BF16)] * 5,
        pltpu.VMEM((K, 1), F32),
        *[pltpu.VMEM((K, K), F32)] * 2,
        pltpu.VMEM((LEV, K, CELLS), F32),
        pltpu.VMEM((LEV - 1, K, CELLS), F32),
        pltpu.SemaphoreType.DMA((3,)),
        *[pltpu.SemaphoreType.DMA((2,))] * 2,
        *[pltpu.SemaphoreType.DMA((LEV,))] * 2,
        pltpu.SemaphoreType.DMA((2 * LEV,)),
        *[pltpu.SemaphoreType.DMA((LEV,))] * 2,
    ]
    vmem = pl.BlockSpec(memory_space=pltpu.VMEM)
    whole = pl.BlockSpec(memory_space=pl.ANY)
    smem = pl.BlockSpec(memory_space=pltpu.SMEM)
    most, last = pl.pallas_call(
        kernel,
        out_shape=(pltpu.VMEM((LEV - 1, ROWS, MINE, WIDE), F32), pltpu.VMEM((K, CELLS), F32)),
        in_specs=[whole, whole, smem, vmem, vmem],
        out_specs=(vmem, vmem),
        scratch_shapes=scratch,
        compiler_params=pltpu.CompilerParams(
            collective_id=0, has_side_effects=True, vmem_limit_bytes=56 * 1024 * 1024),
        name="analysis",
    )(ensemble, kappa, advect, observed.reshape(LEV, 1, CELLS), counts.reshape(LEV, 1, CELLS))
    return pl.pallas_call(
        members_first,
        out_shape=jax.ShapeDtypeStruct((MINE, LEV, ROWS, WIDE), F32),
        in_specs=[whole, vmem],
        out_specs=whole,
        scratch_shapes=[pltpu.VMEM((ROWS, MINE, WIDE), F32), pltpu.SemaphoreType.DMA((2,))],
        compiler_params=pltpu.CompilerParams(vmem_limit_bytes=4 * 1024 * 1024),
        name="members_first",
    )(most, last)


def solution(mesh):
    in_specs = (
        P("member", None, None, "tile"),
        P(None, None, "tile"),
        P(),
        P(None, "member", "tile", None),
        P(None, "member", "tile", None),
    )
    return jax.shard_map(
        on_device, mesh=mesh, in_specs=in_specs, out_specs=P("member", None, None, "tile"), check_vma=False
    )
```

```python
import jax
import jax.numpy as jnp
from jax import lax
from jax.experimental import pallas as pl
from jax.experimental.pallas import tpu as pltpu
from jax.sharding import PartitionSpec as P

MESH = pl.DeviceIdType.MESH
F32 = jnp.float32
BF16 = jnp.bfloat16
LEV = 4
ROWS = 32
PAD = ROWS + 2
WIDE = 384
CELLS = 768
COLS = 48
LANES = 128
MINE = 16
FIELDS = 24
CHUNK = 256
K = 256
PEERS = 16
TILES = 8
ITERS = 10


def loop(count, body):
    def step(i, carry):
        body(i)
        return carry

    lax.fori_loop(0, count, step, 0)


def split3(a):
    a0 = a.astype(BF16)
    rest = a - a0.astype(F32)
    a1 = rest.astype(BF16)
    return a0, a1, (rest - a1.astype(F32)).astype(BF16)


def mm(a, b):
    return jnp.dot(a, b, preferred_element_type=F32)


def mm_t(a, b):
    return lax.dot_general(a, b, (((1,), (1,)), ((), ())), preferred_element_type=F32)


def product(a, b):
    return mm(a[0], b[0]) + (
        (mm(a[0], b[1]) + mm(a[1], b[0]))
        + (mm(a[1], b[1]) + mm(a[0], b[2]) + mm(a[2], b[0]))
    )


def sheared(arrays):
    lane = lax.broadcasted_iota(jnp.int32, (MINE, LANES), 1)
    result = []
    for d in range(8):
        parts = []
        for t in range(3):
            low, high = LANES * t, LANES * (t + 1)
            first, last = low // COLS, (high - 1) // COLS
            here = [arrays[(p - d) % 8][:, low:high] for p in range(first, last + 1)]
            value = here[-1]
            for p in range(last - 1, first - 1, -1):
                value = jnp.where(lane < COLS * (p + 1) - low, here[p - first], value)
            parts.append(value)
        result.append(jnp.concatenate(parts, axis=1))
    return result


def turned(array, shift):
    shift %= array.shape[1]
    return pltpu.roll(array, shift, 1) if shift else array


def moved(here, east, west, north, south, kappa, speed):
    return here + kappa * (east + west + north + south - 4.0 * here) + speed * (west - here)


def unpack(patches_ref, rows_ref, r):
    for h in range(2):
        patches = [
            patches_ref[pl.ds(pl.multiple_of((r * 8 + c) * MINE, MINE), MINE), WIDE * h:WIDE * (h + 1)]
            for c in range(8)
        ]
        for i, row in enumerate(sheared(patches)):
            rows_ref[16 * r + 8 * h + i] = turned(row, -COLS * i)


def kernel(
    ens, kap, adv, obs, cnt, field, last,
    ensv, kapv, head, tail, send_w, send_e, recv_e, recv_w, mend_w, mend_e, u1,
    snd, rcv, ph, pm, pl_, qh, ql, drive, inv, root, ana, ret,
    in_sem, halo_ss, halo_rs, fwd_ss, fwd_rs, own_sem, back_ss, back_rs,
):
    me = lax.axis_index("member")
    tile = lax.axis_index("tile")
    east = lax.rem(tile + 1, TILES)
    west = lax.rem(tile + TILES - 1, TILES)
    inner = pl.ds(1, ROWS)

    def load_levels(part, base, count):
        levels = pl.ds(base, count)

        def member(m):
            pltpu.make_async_copy(
                ens.at[m, levels], ensv.at[levels, inner, m, :], in_sem.at[part]).start()

        loop(MINE, member)

    barrier = pltpu.get_barrier_semaphore()

    def greet(k):
        peer = lax.rem(me + k + 1, PEERS)
        pl.semaphore_signal(barrier, inc=1, device_id={"member": peer}, device_id_type=MESH)

    loop(PEERS - 1, greet)
    for side in (east, west):
        pl.semaphore_signal(barrier, inc=1, device_id={"tile": side}, device_id_type=MESH)

    load_kappa = pltpu.make_async_copy(kap, kapv, in_sem.at[2])
    load_kappa.start()
    load_levels(0, 0, 1)

    load_levels(1, 1, LEV - 1)

    def clear(l):
        for y in (0, ROWS + 1):
            ensv[l, y] = jnp.zeros((FIELDS, WIDE), F32)
            u1[l, y] = jnp.zeros((MINE, WIDE), F32)

    loop(LEV, clear)

    def wait_bytes(ref, sem):
        pltpu.make_async_copy(ref, ref, sem).wait()

    def spread_kappa(j):
        l, b = j // 4, lax.rem(j, 4)
        rows = kapv[l, pl.ds(pl.multiple_of(8 * b, 8), 8), :]
        for i in range(8):
            ensv[l, 8 * b + i + 1, MINE:FIELDS] = jnp.broadcast_to(rows[i:i + 1], (FIELDS - MINE, WIDE))

    load_kappa.wait()
    loop(4, spread_kappa)
    wait_bytes(ensv.at[pl.ds(0, 1), inner, 0:MINE], in_sem.at[0])

    def advanced(source, count, l, r):
        rows = [source[l, 16 * r + i, 0:count] for i in range(18)]
        speed = adv[l]
        result = []
        for i in range(16):
            south, here, north = rows[i:i + 3]
            kappa = ensv[l, 16 * r + i + 1, MINE:FIELDS]
            kappa = jnp.concatenate([kappa, kappa], axis=0)
            result.append(moved(here, turned(here, -1), turned(here, 1), north, south, kappa, speed))
        return result

    def step_one(l, r):
        for i, row in enumerate(advanced(ensv, MINE, l, r)):
            u1[l, 16 * r + i + 1] = row

    def step_two(l, r):
        rows = advanced(u1, MINE, l, r)
        for h in range(2):
            done = [turned(rows[8 * h + i], COLS * i) for i in range(8)]
            for c, patch in enumerate(sheared(done)):
                snd[l, r * 8 + c, :, WIDE * h:WIDE * (h + 1)] = patch

    loop(2, lambda r: step_one(0, r))
    loop(2, lambda r: step_two(0, r))
    loop(4 * LEV - 4, lambda j: spread_kappa(j + 4))
    wait_bytes(ensv.at[pl.ds(1, LEV - 1), inner, 0:MINE], in_sem.at[1])

    lane = lax.broadcasted_iota(jnp.int32, (FIELDS, LANES), 1)

    def edges_of(j):
        for l in (2 * j, 2 * j + 1):
            first = jnp.zeros((FIELDS, LANES), F32)
            last = jnp.zeros((FIELDS, LANES), F32)
            for y in range(ROWS):
                ends = jnp.where(lane < 64, ensv[l, y + 1, :, 0:LANES], ensv[l, y + 1, :, 2 * LANES:3 * LANES])
                ends = turned(ends, 4 * y)
                first = jnp.where(lane // 4 == y, ends, first)
                last = jnp.where(lane // 4 == (y - 1) % ROWS, ends, last)
            head[l] = first
            tail[l] = turned(last, 4)

    loop(LEV // 2, edges_of)
    for j in range(LEV // 2):
        send_w[j] = jnp.where(lane % 4 < 2, head[2 * j], turned(head[2 * j + 1], 2))
        send_e[j] = jnp.where(lane % 4 < 2, turned(tail[2 * j + 1], -2), tail[2 * j])
    pl.semaphore_wait(barrier, PEERS + 1)

    to_west = pltpu.make_async_remote_copy(
        send_w, recv_e, halo_ss.at[0], halo_rs.at[0], device_id={"tile": west}, device_id_type=MESH)
    to_east = pltpu.make_async_remote_copy(
        send_e, recv_w, halo_ss.at[1], halo_rs.at[1], device_id={"tile": east}, device_id_type=MESH)
    to_west.start()
    to_east.start()

    def forward(l, peer):
        return pltpu.make_async_remote_copy(
            snd.at[l, peer], rcv.at[l, pl.ds(me * MINE, MINE), :], fwd_ss.at[l], fwd_rs.at[l],
            device_id={"member": peer}, device_id_type=MESH)

    def forward_own(l):
        return pltpu.make_async_copy(snd.at[l, me], rcv.at[l, pl.ds(me * MINE, MINE), :], own_sem.at[l])

    def send_back(l, target):
        mine = pl.ds(me * MINE, MINE)
        pltpu.make_async_copy(ana.at[l, mine, :], target.at[mine, :], own_sem.at[LEV + l]).start()

        def one(k):
            peer = lax.rem(me + k + 1, PEERS)
            pltpu.make_async_remote_copy(
                ana.at[l, pl.ds(peer * MINE, MINE), :], target.at[mine, :], back_ss.at[l], back_rs.at[l],
                device_id={"member": peer}, device_id_type=MESH).start()

        loop(PEERS - 1, one)

    def wait_back(l, target):
        wait_bytes(target.at[pl.ds(0, MINE), :], own_sem.at[LEV + l])
        wait_bytes(target.at[pl.ds(0, K - MINE), :], back_rs.at[l])

    def send(l, wanted):
        def one(k):
            peer = lax.rem(me + k, PEERS)
            column = lax.rem(peer, 8)
            outer = jnp.logical_or(column == 0, column == 7)

            @pl.when(outer if wanted else jnp.logical_not(outer))
            def _():
                @pl.when(k == 0)
                def _():
                    forward_own(l).start()

                @pl.when(k > 0)
                def _():
                    forward(l, peer).start()

        loop(PEERS, one)

    def compact(a, b, ka, kb, speed, want_a, want_b):
        place = lax.broadcasted_iota(jnp.int32, a.shape, 1)
        slot = place % 4

        def sides(x):
            south = jnp.where(place < 4, 0.0, pltpu.roll(x, 4, 1))
            north = jnp.where(place >= LANES - 4, 0.0, pltpu.roll(x, LANES - 4, 1))
            return north, south

        new_a = new_b = None
        if want_a:
            after = jnp.where(slot == 3, pltpu.roll(b, 3, 1), pltpu.roll(a, LANES - 1, 1))
            new_a = moved(a, after, pltpu.roll(a, 1, 1), *sides(a), ka, speed)
        if want_b:
            before = jnp.where(slot == 0, pltpu.roll(a, LANES - 3, 1), pltpu.roll(b, 1, 1))
            new_b = moved(b, pltpu.roll(b, LANES - 1, 1), before, *sides(b), kb, speed)
        return new_a, new_b

    def mend_edges(l):
        speed = adv[l]

        def parts(both):
            kappa = both[MINE:FIELDS]
            return both[0:MINE], jnp.concatenate([kappa, kappa], axis=0)

        from_west, from_east = recv_w[l // 2], recv_e[l // 2]
        if l % 2:
            from_west, from_east = turned(from_west, 2), turned(from_east, -2)
        (a, ka), (b, kb) = parts(from_west), parts(head[l])
        a, b = compact(a, b, ka, kb, speed, True, True)
        mend_w[l] = compact(a, b, ka, kb, speed, False, True)[1]
        (a, ka), (b, kb) = parts(tail[l]), parts(from_east)
        a, b = compact(a, b, ka, kb, speed, True, True)
        mend_e[l] = compact(a, b, ka, kb, speed, True, False)[0]

    def insert_edges(l):
        place = lax.broadcasted_iota(jnp.int32, (MINE, LANES), 1)
        for mend, c, cell in ((mend_w, 0, 0), (mend_e, 7, COLS - 2)):
            values = mend[l]
            for b in range(4):
                r, h = divmod(b, 2)
                tiles = [snd[l, r * 8 + c, :, WIDE * h + LANES * t:WIDE * h + LANES * (t + 1)] for t in range(3)]
                for i in range(8):
                    to = COLS * ((c + i) % 8) + cell
                    t, to = divmod(to, LANES)
                    source = 4 * (8 * b + i) + (2 if cell else 0)
                    value = turned(values, to - source)
                    tiles[t] = jnp.where(jnp.logical_or(place == to, place == to + 1), value, tiles[t])
                for t in range(3):
                    snd[l, r * 8 + c, :, WIDE * h + LANES * t:WIDE * h + LANES * (t + 1)] = tiles[t]

    def two_steps(l, follow):
        def body(r):
            step_two(l, r)
            if follow:
                step_one(l + 1, r)

        loop(2, body)

    def finish_edges(l):
        mend_edges(l)
        insert_edges(l)
        send(l, True)

    send(0, False)
    loop(2, lambda r: step_one(1, r))
    two_steps(1, True)
    send(1, False)
    two_steps(2, True)
    to_west.wait()
    to_east.wait()
    finish_edges(0)
    finish_edges(1)
    send(2, False)
    finish_edges(2)
    two_steps(3, False)
    send(3, False)
    finish_edges(3)

    order = COLS * lax.rem(me, 8)

    def ordered(row):
        row = jnp.broadcast_to(row, (8, CELLS))
        return jnp.concatenate(
            [pltpu.roll(row[:, WIDE * h:WIDE * (h + 1)], order, 1) for h in range(2)], axis=1)[0:1]

    def analyse(l):
        forward_own(l).wait()
        wait_bytes(rcv.at[l, pl.ds(0, K - MINE), :], fwd_rs.at[l])
        total = jnp.zeros((8, CELLS), F32)

        def add_rows(i, total):
            block = rcv[l, pl.ds(pl.multiple_of(i * CHUNK, CHUNK), CHUNK), :]
            return total + jnp.sum(block.reshape(CHUNK // 8, 8, CELLS), axis=0)

        total = lax.fori_loop(0, K // CHUNK, add_rows, total)
        mean = jnp.sum(total, axis=0, keepdims=True) * (1.0 / K)
        prec = ordered(cnt[l].astype(F32)) * 0.25
        weight = prec * (ordered(obs[l]) - mean) * (1.0 / (K - 1))

        def centre(i):
            at = pl.ds(pl.multiple_of(i * CHUNK, CHUNK), CHUNK)
            block = rcv[l, at, :] - mean
            p0, p1, p2 = split3(block)
            ph[at, :] = p0
            pm[at, :] = p1
            pl_[at, :] = p2
            scaled = block * prec
            q0 = scaled.astype(BF16)
            qh[at, :] = q0
            ql[at, :] = (scaled - q0.astype(F32)).astype(BF16)
            drive[at, :] = jnp.sum(block * weight, axis=1, keepdims=True)

        loop(K // CHUNK, centre)

        gram = mm_t(qh[...], ph[...]) + (mm_t(qh[...], pm[...]) + mm_t(ql[...], ph[...]))
        eye = jnp.where(
            lax.broadcasted_iota(jnp.int32, (K, K), 0) == lax.broadcasted_iota(jnp.int32, (K, K), 1), 1.0, 0.0)
        system = eye + gram * (1.0 / (K - 1))
        scale = jnp.sqrt(jnp.sum(jnp.sum(system * system, axis=1, keepdims=True), axis=0, keepdims=True))
        first = system * (1.0 / scale)
        factor = 1.5 * eye - 0.5 * first
        inv[...] = factor
        root[...] = product(split3(first), split3(factor))

        def newton(i):
            held, base = split3(inv[...]), split3(root[...])
            factor = split3(1.5 * eye - 0.5 * product(held, base))
            inv[...] = product(factor, held)
            root[...] = product(base, factor)

        loop(ITERS - 2, newton)
        held, base = split3(inv[...]), split3(root[...])
        factor = split3(1.5 * eye - 0.5 * product(held, base))
        half = product(factor, held) * lax.rsqrt(scale)

        once = jnp.sum(half * drive[...], axis=0, keepdims=True)
        twice = jnp.sum(half * once, axis=1, keepdims=True)
        w0, w1, w2 = split3(half + jnp.sum(eye * twice, axis=0, keepdims=True))
        for c in range(3):
            at = slice(256 * c, 256 * (c + 1))
            cells = (ph[:, at], pm[:, at], pl_[:, at])
            ana[l, :, at] = mean[:, at] + product((w0, w1, w2), cells)

        @pl.when(l < LEV - 1)
        def _():
            send_back(l, ret.at[l])

        @pl.when(l == LEV - 1)
        def _():
            send_back(l, last)

    loop(LEV, analyse)

    def drain(l):
        wait_bytes(snd.at[l, pl.ds(0, PEERS - 1)], fwd_ss.at[l])
        wait_bytes(ana.at[l, pl.ds(0, K - MINE), :], back_ss.at[l])

    def finish(l):
        wait_back(l, ret.at[l])
        loop(2, lambda r: unpack(ret.at[l], field.at[l], r))
        drain(l)

    loop(LEV - 1, finish)
    drain(LEV - 1)
    wait_back(LEV - 1, last)


def members_first(field, last, out, spare, sems):
    early = pl.ds(0, LEV - 1)
    loop(MINE, lambda m: pltpu.make_async_copy(field.at[:, :, m, :], out.at[m, early], sems.at[0]).start())
    loop(2, lambda r: unpack(last, spare, r))
    loop(MINE, lambda m: pltpu.make_async_copy(spare.at[:, m, :], out.at[m, LEV - 1], sems.at[1]).start())
    pltpu.make_async_copy(field, field, sems.at[0]).wait()
    pltpu.make_async_copy(spare, spare, sems.at[1]).wait()


def on_device(ensemble, kappa, advect, observed, counts):
    scratch = [
        pltpu.VMEM((LEV, PAD, FIELDS, WIDE), F32),
        pltpu.VMEM((LEV, ROWS, WIDE), F32),
        *[pltpu.VMEM((LEV, FIELDS, LANES), F32)] * 2,
        *[pltpu.VMEM((LEV // 2, FIELDS, LANES), F32)] * 4,
        *[pltpu.VMEM((LEV, MINE, LANES), F32)] * 2,
        pltpu.VMEM((LEV, PAD, MINE, WIDE), F32),
        pltpu.VMEM((LEV, PEERS, MINE, CELLS), F32),
        pltpu.VMEM((LEV, K, CELLS), F32),
        *[pltpu.VMEM((K, CELLS), BF16)] * 5,
        pltpu.VMEM((K, 1), F32),
        *[pltpu.VMEM((K, K), F32)] * 2,
        pltpu.VMEM((LEV, K, CELLS), F32),
        pltpu.VMEM((LEV - 1, K, CELLS), F32),
        pltpu.SemaphoreType.DMA((3,)),
        *[pltpu.SemaphoreType.DMA((2,))] * 2,
        *[pltpu.SemaphoreType.DMA((LEV,))] * 2,
        pltpu.SemaphoreType.DMA((2 * LEV,)),
        *[pltpu.SemaphoreType.DMA((LEV,))] * 2,
    ]
    vmem = pl.BlockSpec(memory_space=pltpu.VMEM)
    whole = pl.BlockSpec(memory_space=pl.ANY)
    smem = pl.BlockSpec(memory_space=pltpu.SMEM)
    most, last = pl.pallas_call(
        kernel,
        out_shape=(pltpu.VMEM((LEV - 1, ROWS, MINE, WIDE), F32), pltpu.VMEM((K, CELLS), F32)),
        in_specs=[whole, whole, smem, vmem, vmem],
        out_specs=(vmem, vmem),
        scratch_shapes=scratch,
        compiler_params=pltpu.CompilerParams(
            collective_id=0, has_side_effects=True, vmem_limit_bytes=56 * 1024 * 1024),
        name="analysis",
    )(ensemble, kappa, advect, observed.reshape(LEV, 1, CELLS), counts.reshape(LEV, 1, CELLS))
    return pl.pallas_call(
        members_first,
        out_shape=jax.ShapeDtypeStruct((MINE, LEV, ROWS, WIDE), F32),
        in_specs=[whole, vmem],
        out_specs=whole,
        scratch_shapes=[pltpu.VMEM((ROWS, MINE, WIDE), F32), pltpu.SemaphoreType.DMA((2,))],
        compiler_params=pltpu.CompilerParams(vmem_limit_bytes=4 * 1024 * 1024),
        name="members_first",
    )(most, last)


def solution(mesh):
    in_specs = (
        P("member", None, None, "tile"),
        P(None, None, "tile"),
        P(),
        P(None, "member", "tile", None),
        P(None, "member", "tile", None),
    )
    return jax.shard_map(
        on_device, mesh=mesh, in_specs=in_specs, out_specs=P("member", None, None, "tile"), check_vma=False
    )
```
